32 devices in a mesh: gx: 4 (over x, core), gy: 8 (over z, y).
Axes of the slice: x: 2, y: 2, z: 4, core: 2. Of those that a mesh axis runs over, the one named last changes fastest.
Arguments:
- point_coords: float32 [3, 524288], P(None, ('gx', 'gy')), may hold values from -1 to 1
- strengths: float32 [3, 524288], P(None, ('gx', 'gy')), may hold values from -0.06 to 0.06
- centers: float32 [3, 512], replicated, may hold values from 0 to 0.3
- half_widths: float32 [512], replicated, may hold values from 0.1 to 0.3
- tile_source: int32 [32, 128], P(('gx', 'gy')), may hold values from 0 to 511, as said below
- tile_target: int32 [32, 128], P(('gx', 'gy')), may hold values from 0 to 511, as said below
- tile_count: int32 [32], P(('gx', 'gy')), may hold values from 1 to 128, as said below
Outputs:
- velocity: float32 [3, 524288], P(None, ('gx', 'gy'))
The draws below stay inside these ranges and needn't reach their ends.
Inputs may be any that keep to these rules, and one draw needn't show every extreme that they name: `tile_source`: cluster c belongs to domain c // 16. Among the first tile_count[d] entries of row d at most 4 name clusters of any one domain, and some domain reaches 4; later entries are valid ids of no interaction. `tile_target`: cluster c belongs to domain c // 16. Among the first tile_count[d] entries of row d at most 4 name clusters of any one domain, and some domain reaches 4; later entries are valid ids of no interaction. `tile_count`: 128 on at least one domain.
All inputs are finite; a program needn't handle non-finite values.
Results may differ from the reference program's by a relative error of at most 0.0001.
Values sent between devices are 32-bit elements; how exact they have to be, the bound alone decides.
A program may use at most 64 MiB of HBM per device.

```python
import math
import jax
import jax.numpy as jnp
from jax import lax

CL_DEV = 16
PTS = 1024
DEG = 7
TILES_DEV = 128
Q = 512
DOMAINS = 32
CAP = 4
SLOTS = 128
CLUSTERS = 512
POINTS = 524288


def tile_tables(key):
    base_key = jax.random.fold_in(key, 4111)
    shift_key, fullest_key, source_key, target_key, source_local, target_local = jax.random.split(base_key, 6)
    shifts = jax.random.randint(shift_key, (DOMAINS,), 0, 4)
    totals = jnp.right_shift(jnp.full((DOMAINS,), TILES_DEV, jnp.int32), shifts)
    totals = jnp.maximum(totals, 1)
    fullest = jax.random.randint(fullest_key, (), 0, DOMAINS)
    totals = jnp.where(jnp.arange(DOMAINS) == fullest, TILES_DEV, totals).astype(jnp.int32)

    def owner_rows(owner_key):
        row_keys = jax.random.split(owner_key, DOMAINS)
        orders = jax.vmap(lambda row_key: jax.random.permutation(row_key, SLOTS))(row_keys)
        return orders[:, :TILES_DEV] // CAP
    sources = owner_rows(source_key) * CL_DEV + jax.random.randint(source_local, (DOMAINS, TILES_DEV), 0, CL_DEV)
    targets = owner_rows(target_key) * CL_DEV + jax.random.randint(target_local, (DOMAINS, TILES_DEV), 0, CL_DEV)
    return (sources.astype(jnp.int32), targets.astype(jnp.int32), totals)


def draw_tile_source(key, part):
    return tile_tables(key)[0]


def draw_tile_target(key, part):
    return tile_tables(key)[1]


def draw_tile_count(key, part):
    return tile_tables(key)[2]


def block_scale(own_key, dims, cuts, least, largest):
    level = 1.0
    for position, blocks in cuts:
        draws = jax.random.uniform(jax.random.fold_in(jax.random.fold_in(own_key, 6), position), (blocks,), jnp.float32, least / len(cuts), largest / len(cuts))
        level = level * jnp.repeat(jnp.exp(draws), dims[position] // blocks).reshape((-1,) + (1,) * (len(dims) - 1 - position))
    return level


def scatter_about(own_key, extent, deviation, reach, cuts=(), kind=jnp.bfloat16):
    array = jax.random.normal(own_key, extent, jnp.float32) * deviation
    if len(cuts) > 0:
        array = block_scale(own_key, extent, cuts, -0.22, 0.18) * array
    return jnp.clip(array, min=-reach, max=reach).astype(kind)


def setup_inputs(seed: int = 0) -> dict:
    streams_of = jax.random.split(jax.random.key(seed), 8)
    return {
        "point_coords": jnp.clip(jax.random.uniform(streams_of[0], (3, POINTS), jnp.float32, -1.0, 1.0) * block_scale(streams_of[0], (3, POINTS), ((1, 32),), -0.4, 0.0), -1.0, 1.0),
        "strengths": scatter_about(streams_of[1], (3, POINTS), 0.01, 0.06, ((1, 32),), jnp.float32),
        "centers": jnp.clip(jax.random.uniform(streams_of[2], (3, CLUSTERS), jnp.float32, 0.0, 0.3), 0.0, 0.3),
        "half_widths": jnp.clip(jnp.exp(jax.random.uniform(streams_of[3], (CLUSTERS,), jnp.float32, math.log(0.1), math.log(0.3))), 0.1, 0.3),
        "tile_source": draw_tile_source(jax.random.fold_in(streams_of[7], 71), 0),
        "tile_target": draw_tile_target(jax.random.fold_in(streams_of[7], 71), 0),
        "tile_count": draw_tile_count(jax.random.fold_in(streams_of[7], 71), 0),
    }


smoothing_sq = 0.01
biot_factor = -0.07957747154594767

def chebyshev(degree):
    counter = jnp.arange(degree + 1, dtype=jnp.float32)
    return jnp.cos(jnp.pi * counter / degree)

def lagrange(points, cheb_nodes):
    node_count = cheb_nodes.shape[0]
    differ = points[None, :] - cheb_nodes[:, None]
    diagonal = jnp.eye(node_count, dtype=bool)
    numerator = jnp.prod(jnp.where(diagonal[:, :, None], 1.0, differ[None, :, :]), axis=1)
    spacing = cheb_nodes[:, None] - cheb_nodes[None, :]
    denominator = jnp.prod(jnp.where(diagonal, 1.0, spacing), axis=1)
    return numerator / denominator[:, None]

def basis_parts(coords, cheb_nodes):
    basis_x = lagrange(coords[0], cheb_nodes)
    basis_y = lagrange(coords[1], cheb_nodes)
    basis_z = lagrange(coords[2], cheb_nodes)
    node_count = cheb_nodes.shape[0]
    paired = (basis_y[:, None, :] * basis_z[None, :, :]).reshape(node_count * node_count, -1)
    return (basis_x, paired)

def upward(coords, weights, cheb_nodes):
    basis_x, paired = basis_parts(coords, cheb_nodes)
    weighted = weights[:, None, :] * paired[None, :, :]
    charge = jnp.einsum('ai,cei->cae', basis_x, weighted, precision=lax.Precision.HIGHEST)
    return charge.reshape(3, -1)

def downward(coords, proxy_values, cheb_nodes):
    basis_x, paired = basis_parts(coords, cheb_nodes)
    node_count = cheb_nodes.shape[0]
    shaped = proxy_values.reshape(3, node_count, node_count * node_count)
    spread = jnp.einsum('cae,ai->cei', shaped, basis_x, precision=lax.Precision.HIGHEST)
    return lax.optimization_barrier(jnp.sum(spread * paired[None, :, :], axis=1))

def proxy_grid(center, half_width, cheb_nodes):
    node_count = cheb_nodes.shape[0]
    cube_shape = (node_count, node_count, node_count)
    along_x = jnp.broadcast_to(cheb_nodes[:, None, None], cube_shape).reshape(-1)
    along_y = jnp.broadcast_to(cheb_nodes[None, :, None], cube_shape).reshape(-1)
    along_z = jnp.broadcast_to(cheb_nodes[None, None, :], cube_shape).reshape(-1)
    return center[:, None] + half_width * jnp.stack([along_x, along_y, along_z])

def tile_velocity(target_grid, source_grid, charge):
    offset = target_grid[:, None, :] - source_grid[:, :, None]
    radius_sq = lax.optimization_barrier(jnp.sum(offset * offset, axis=0)) + smoothing_sq
    kernel = 1.0 / (radius_sq * jnp.sqrt(radius_sq))
    velocity_x = lax.optimization_barrier(jnp.sum(kernel * (offset[1] * charge[2][:, None] - offset[2] * charge[1][:, None]), axis=0))
    velocity_y = lax.optimization_barrier(jnp.sum(kernel * (offset[2] * charge[0][:, None] - offset[0] * charge[2][:, None]), axis=0))
    velocity_z = lax.optimization_barrier(jnp.sum(kernel * (offset[0] * charge[1][:, None] - offset[1] * charge[0][:, None]), axis=0))
    return biot_factor * jnp.stack([velocity_x, velocity_y, velocity_z])

def reference(point_coords, strengths, centers, half_widths, tile_source, tile_target, tile_count):
    cheb_nodes = chebyshev(DEG)
    coords = point_coords.reshape(3, CLUSTERS, PTS).transpose(1, 0, 2)
    weights = strengths.reshape(3, CLUSTERS, PTS).transpose(1, 0, 2)
    charges = lax.map(lambda pieces: upward(pieces[0], pieces[1], cheb_nodes), (coords, weights))
    proxy_grids = jax.vmap(lambda center, half_width: proxy_grid(center, half_width, cheb_nodes))(centers.T, half_widths)
    alive_mask = (jnp.arange(TILES_DEV)[None, :] < tile_count[:, None]).astype(jnp.float32).reshape(-1, 8)
    sources = tile_source.reshape(-1, 8)
    targets = tile_target.reshape(-1, 8)

    def add_group(totals, tile_group):
        source_ids, target_ids, alive_rows = tile_group
        contributions = jax.vmap(tile_velocity)(proxy_grids[target_ids], proxy_grids[source_ids], charges[source_ids])
        return (totals.at[target_ids].add(contributions * alive_rows[:, None, None]), None)
    empty_totals = jnp.zeros((CLUSTERS, 3, Q), jnp.float32)
    totals, _ = lax.scan(add_group, empty_totals, (sources, targets, alive_mask))
    velocity = lax.map(lambda pieces: downward(pieces[0], pieces[1], cheb_nodes), (coords, totals))
    return velocity.transpose(1, 0, 2).reshape(3, POINTS)
```

```python
import functools

import jax
import jax.numpy as jnp
import numpy as np
from jax import lax
from jax.experimental import pallas as pl
from jax.experimental.pallas import tpu as pltpu
from jax.sharding import PartitionSpec as P

CL_DEV = 16
PTS = 1024
DEG = 7
TILES_DEV = 128
AXES = ("gx", "gy")

NODES = DEG + 1
PLANE = NODES * NODES
PROXIES = NODES**3
LANES = 128
GROUPS = PROXIES // LANES
CHARGE_ROWS = CL_DEV * 3 * GROUPS
ROWS = CHARGE_ROWS + 8
smoothing_sq = 0.01
biot_factor = -0.07957747154594767

CHEB = np.cos(np.pi * np.arange(NODES) / DEG)
EVEN_ODD = [0, 2, 4, 6, 1, 3, 5, 7]
VMEM = pl.BlockSpec(memory_space=pltpu.VMEM)
SMEM = pl.BlockSpec(memory_space=pltpu.SMEM)


def basis_table(order):
    table = np.zeros((NODES, NODES, LANES), np.float32)
    for row, a in enumerate(order):
        others = [m for m in range(NODES) if m != a]
        for j, m in enumerate(others):
            table[j, row, :] = CHEB[m]
        table[DEG, row, :] = 1.0 / np.prod([CHEB[a] - CHEB[m] for m in others])
    return table


BASIS = basis_table(range(NODES))
BASIS_EVEN_ODD = basis_table(EVEN_ODD)


def lane_tables():
    k = np.arange(PROXIES)
    table = np.zeros((16, PROXIES), np.float32)
    table[0] = CHEB[k // PLANE]
    table[1] = CHEB[(k // NODES) % NODES]
    table[2] = CHEB[k % NODES]
    table[8:16] = CHEB[:, None]
    return table


def plane_tables():
    rows = np.arange(PLANE)
    along_y = np.repeat(CHEB[rows // NODES][:, None], LANES, axis=1)
    along_z = np.repeat(CHEB[rows % NODES][:, None], LANES, axis=1)
    return np.concatenate([along_y, along_z], axis=1).astype(np.float32)


def lagrange(row, table_ref):
    repeats = row.shape[1] // LANES

    def column(j):
        return jnp.concatenate([table_ref[j]] * repeats, axis=1)

    value = (row - column(0)) * column(DEG)
    for j in range(1, DEG):
        value = value * (row - column(j))
    return value


def split(value):
    high = value.astype(jnp.bfloat16)
    low = (value - high.astype(jnp.float32)).astype(jnp.bfloat16)
    return high, low


def paired_basis(basis_y, basis_z):
    return jnp.concatenate([basis_y[b : b + 1, :] * basis_z for b in range(NODES)], axis=0)


def up_kernel(count_ref, coords_ref, weights_ref, source_ref, target_ref, basis_ref, mixed_ref, out_ref):
    lane = lax.broadcasted_iota(jnp.int32, (NODES, LANES), 1)
    row = lax.broadcasted_iota(jnp.int32, (NODES, LANES), 0)
    low_lanes = lane < PLANE

    def cluster(c):
        at = pl.ds(pl.multiple_of(c * PTS, PTS), PTS)
        basis_x = lagrange(coords_ref[0:1, at], mixed_ref)
        basis_y = lagrange(coords_ref[1:2, at], basis_ref)
        basis_z = lagrange(coords_ref[2:3, at], basis_ref)
        left = jnp.concatenate([weights_ref[i : i + 1, at] * basis_x for i in range(3)], axis=0)
        left_rest = left - left.astype(jnp.bfloat16).astype(jnp.float32)
        left = jnp.concatenate([left, left_rest], axis=0).astype(jnp.bfloat16)
        right = jnp.concatenate(split(paired_basis(basis_y, basis_z)), axis=0)
        product = lax.dot_general(
            left, right, (((1,), (1,)), ((), ())), preferred_element_type=jnp.float32
        )
        both = product[: 3 * NODES] + product[3 * NODES :]
        return both + pltpu.roll(both, PLANE, 1)

    def pair(p, carry):
        first = cluster(2 * p)
        second = cluster(2 * p + 1)
        for i in range(3):
            one = first[i * NODES : (i + 1) * NODES]
            two = second[i * NODES : (i + 1) * NODES]
            one = jnp.where(low_lanes, one, pltpu.roll(one, 4, 0))
            two = jnp.where(low_lanes, pltpu.roll(two, 4, 0), two)
            at = pl.ds(pl.multiple_of(p * 24 + i * 8, 8), 8)
            out_ref[at, :] = jnp.where(row < 4, one, two)
        return carry

    lax.fori_loop(0, CL_DEV // 2, pair, 0)
    source = source_ref[...]
    target = target_ref[...]
    owner = lax.shift_right_logical(target, 4)
    payload = (source * CL_DEV + (target - owner * CL_DEV)).astype(jnp.float32)
    alive = lax.broadcasted_iota(jnp.int32, (1, TILES_DEV), 1) < count_ref[0]
    owner = jnp.where(alive, owner, -1).astype(jnp.float32)
    out_ref[CHARGE_ROWS:, :] = jnp.where(row == 0, payload, jnp.where(row == 1, owner, 0.0))


def table_kernel(capacity, me_ref, rows_ref, out_ref):
    domains = rows_ref.shape[0]
    rows = rows_ref[...]
    payload = jnp.concatenate([rows[d, 0:1, :] for d in range(domains)], axis=0)
    owner = jnp.concatenate([rows[d, 1:2, :] for d in range(domains)], axis=0)
    mine = owner == me_ref[0].astype(jnp.float32)
    before = lax.broadcasted_iota(jnp.int32, (TILES_DEV, TILES_DEV), 0)
    after = lax.broadcasted_iota(jnp.int32, (TILES_DEV, TILES_DEV), 1)
    earlier = (before < after).astype(jnp.float32).astype(jnp.bfloat16)
    rank = jnp.dot(
        mine.astype(jnp.float32).astype(jnp.bfloat16), earlier, preferred_element_type=jnp.float32
    )
    lane = lax.broadcasted_iota(jnp.int32, (domains, TILES_DEV), 1)
    table = jnp.full((domains, TILES_DEV), -1.0, jnp.float32)
    for r in range(capacity):
        chosen = jnp.where(mine & (rank == float(r)), payload + 1.0, 0.0)
        chosen = jnp.sum(chosen, axis=1, keepdims=True) - 1.0
        table = jnp.where(lane == r, chosen, table)
    out_ref[...] = table.astype(jnp.int32)


def tile_kernel(
    capacity,
    table_ref,
    centers_ref,
    widths_ref,
    charges_ref,
    coords_ref,
    lanes_ref,
    planes_ref,
    basis_ref,
    out_ref,
    list_ref,
    total_ref,
):
    domains = table_ref.shape[0]
    total_ref[...] = jnp.zeros_like(total_ref)

    def collect(d, found):
        for r in range(capacity):
            entry = table_ref[d, r]
            list_ref[found] = entry
            found = found + (entry >= 0).astype(jnp.int32)
        return found

    found = lax.fori_loop(0, domains, collect, jnp.int32(0))
    list_ref[found] = 0

    def tile(j):
        entry = list_ref[j]
        source = lax.shift_right_logical(entry, 4)
        local = lax.bitwise_and(entry, CL_DEV - 1)
        home = lax.shift_right_logical(source, 4)
        within = lax.bitwise_and(source, CL_DEV - 1)
        return entry, source, local, home, within

    def one_tile(j, me):
        _, source, local, home, within = tile(j)
        target = me * CL_DEV + local
        scale = jnp.where(j < found, jnp.float32(biot_factor), jnp.float32(0.0))
        width_t = widths_ref[target]
        width_s = widths_ref[source]
        shift = [centers_ref[i, target] - centers_ref[i, source] for i in range(3)]
        first_row = lax.shift_right_logical(within, 1) * 24 + lax.bitwise_and(within, 1) * 4
        charge = [
            jnp.concatenate(
                [charges_ref[home, pl.ds(first_row + i * 8 + g, 1), :] for g in range(GROUPS)], axis=1
            )
            for i in range(3)
        ]
        unit = [lanes_ref[i : i + 1, :] for i in range(3)]
        near = [width_s * unit[i] for i in range(3)]
        moment = [
            near[1] * charge[2] - near[2] * charge[1],
            near[2] * charge[0] - near[0] * charge[2],
            near[0] * charge[1] - near[1] * charge[0],
        ]
        nothing = jnp.zeros((2, PROXIES), jnp.float32)
        features = jnp.concatenate(charge + moment + [nothing], axis=0)
        rest = features - features.astype(jnp.bfloat16).astype(jnp.float32)
        features = jnp.concatenate([features, rest], axis=0).astype(jnp.bfloat16)
        place = [width_t * unit[i] + shift[i] for i in range(3)]
        along_x = place[0] - width_s * lanes_ref[8:16, :]
        along_x = along_x * along_x
        along_y = place[1][:, :LANES] - width_s * planes_ref[:, :LANES]
        along_z = place[2][:, :LANES] - width_s * planes_ref[:, LANES:]
        plane = along_y * along_y + along_z * along_z + smoothing_sq
        summed = jnp.zeros((16, PROXIES), jnp.float32)
        for half in range(2):
            blocks = []
            for a in range(half * 4, half * 4 + 4):
                radius_sq = jnp.concatenate(
                    [plane + along_x[a : a + 1, g * LANES : (g + 1) * LANES] for g in range(GROUPS)], axis=1
                )
                inverse = lax.rsqrt(radius_sq)
                blocks.append(inverse * inverse * inverse)
            high, low = split(jnp.concatenate(blocks, axis=0))
            part = features[:, half * 256 : (half + 1) * 256]
            summed = summed + jnp.dot(part, high, preferred_element_type=jnp.float32)
            summed = summed + jnp.dot(part, low, preferred_element_type=jnp.float32)
        both = (summed[:8] + summed[8:]) * scale
        s = [both[i : i + 1] for i in range(6)]
        velocity = [
            place[1] * s[2] - place[2] * s[1] - s[3],
            place[2] * s[0] - place[0] * s[2] - s[4],
            place[0] * s[1] - place[1] * s[0] - s[5],
        ]
        return local, velocity

    me = lax.axis_index(AXES)

    def two_tiles(i, carry):
        for local, velocity in [one_tile(2 * i, me), one_tile(2 * i + 1, me)]:
            for n in range(3):
                total_ref[local, n : n + 1, :] += velocity[n]
        return carry

    lax.fori_loop(0, lax.shift_right_logical(found + 1, 1), two_tiles, 0)

    def down(c, carry):
        at = pl.ds(pl.multiple_of(c * PTS, PTS), PTS)
        basis_x = lagrange(coords_ref[0:1, at], basis_ref)
        basis_y = lagrange(coords_ref[1:2, at], basis_ref)
        basis_z = lagrange(coords_ref[2:3, at], basis_ref)
        high, low = split(paired_basis(basis_y, basis_z))
        values = total_ref[c]
        values = jnp.concatenate([values[:, a * PLANE : (a + 1) * PLANE] for a in range(NODES)], axis=0)
        values_high, values_low = split(values)
        spread = jnp.dot(values_high, high, preferred_element_type=jnp.float32)
        spread = spread + jnp.dot(values_low, high, preferred_element_type=jnp.float32)
        spread = spread + jnp.dot(values_high, low, preferred_element_type=jnp.float32)
        velocity = basis_x[0:1, :] * spread[0:8]
        for a in range(1, NODES):
            velocity = velocity + basis_x[a : a + 1, :] * spread[a * 8 : (a + 1) * 8]
        out_ref[:, at] = velocity[:3]
        return carry

    lax.fori_loop(0, CL_DEV, down, 0)


def local(point_coords, strengths, centers, half_widths, tile_source, tile_target, tile_count):
    domains = lax.axis_size(AXES)
    capacity = (TILES_DEV + domains - 1) // domains
    params = pltpu.CompilerParams(vmem_limit_bytes=48 * 1024 * 1024)
    basis = jnp.asarray(BASIS)
    offered = pl.pallas_call(
        up_kernel,
        out_shape=jax.ShapeDtypeStruct((ROWS, LANES), jnp.float32),
        in_specs=[SMEM] + [VMEM] * 6,
        out_specs=VMEM,
        compiler_params=params,
        name="upward",
    )(tile_count, point_coords, strengths, tile_source, tile_target, basis, jnp.asarray(BASIS_EVEN_ODD))
    gathered = lax.all_gather(offered, AXES, axis=0, tiled=False)
    me = lax.axis_index(AXES).astype(jnp.int32).reshape(1)
    table = pl.pallas_call(
        functools.partial(table_kernel, capacity),
        grid=(1,),
        out_shape=jax.ShapeDtypeStruct((domains, TILES_DEV), jnp.int32),
        in_specs=[SMEM, pl.BlockSpec((domains, 8, LANES), lambda i: (0, CHARGE_ROWS // 8, 0))],
        out_specs=pl.BlockSpec((domains, TILES_DEV), lambda i: (0, 0)),
        compiler_params=params,
        name="tables",
    )(me, gathered)
    return pl.pallas_call(
        functools.partial(tile_kernel, capacity),
        out_shape=jax.ShapeDtypeStruct((3, CL_DEV * PTS), jnp.float32),
        in_specs=[SMEM] * 3 + [VMEM] * 5,
        out_specs=VMEM,
        scratch_shapes=[
            pltpu.SMEM((domains * capacity + 8,), jnp.int32),
            pltpu.VMEM((CL_DEV, 8, PROXIES), jnp.float32),
        ],
        compiler_params=params,
        name="tiles",
    )(
        table,
        centers,
        half_widths,
        gathered,
        point_coords,
        jnp.asarray(lane_tables()),
        jnp.asarray(plane_tables()),
        basis,
    )


def solution(mesh):
    return jax.shard_map(
        local,
        mesh=mesh,
        in_specs=(
            P(None, AXES),
            P(None, AXES),
            P(),
            P(),
            P(AXES, None),
            P(AXES, None),
            P(AXES),
        ),
        out_specs=P(None, AXES),
        check_vma=False,
    )
```

```python
import functools

import jax
import jax.numpy as jnp
import numpy as np
from jax import lax
from jax.experimental import pallas as pl
from jax.experimental.pallas import tpu as pltpu
from jax.sharding import PartitionSpec as P

CL_DEV = 16
PTS = 1024
DEG = 7
TILES_DEV = 128
AXES = ("gx", "gy")

NODES = DEG + 1
PLANE = NODES * NODES
PROXIES = NODES**3
LANES = 128
GROUPS = PROXIES // LANES
CHARGE_ROWS = CL_DEV * 3 * GROUPS
ROWS = CHARGE_ROWS + 8
smoothing_sq = 0.01
biot_factor = -0.07957747154594767

CHEB = np.cos(np.pi * np.arange(NODES) / DEG)
EVEN_ODD = [0, 2, 4, 6, 1, 3, 5, 7]
VMEM = pl.BlockSpec(memory_space=pltpu.VMEM)
SMEM = pl.BlockSpec(memory_space=pltpu.SMEM)


def basis_columns(order):
    row = lax.broadcasted_iota(jnp.int32, (NODES, LANES), 0)

    def column(values):
        tile = jnp.full((NODES, LANES), float(values[0]), jnp.float32)
        for n in range(1, NODES):
            tile = jnp.where(row == n, jnp.float32(values[n]), tile)
        return tile

    others = [[m for m in range(NODES) if m != a] for a in order]
    columns = [column([CHEB[left[j]] for left in others]) for j in range(DEG)]
    inverse = [1.0 / np.prod([CHEB[a] - CHEB[m] for m in left]) for a, left in zip(order, others)]
    return columns + [column(inverse)]


def lane_tables():
    k = np.arange(PROXIES)
    table = np.zeros((16, PROXIES), np.float32)
    table[0] = CHEB[k // PLANE]
    table[1] = CHEB[(k // NODES) % NODES]
    table[2] = CHEB[k % NODES]
    table[8:16] = CHEB[:, None]
    return table


def plane_tables():
    rows = np.arange(PLANE)
    along_y = np.repeat(CHEB[rows // NODES][:, None], LANES, axis=1)
    along_z = np.repeat(CHEB[rows % NODES][:, None], LANES, axis=1)
    return np.concatenate([along_y, along_z], axis=1).astype(np.float32)


def lagrange(row, columns):
    repeats = row.shape[1] // LANES

    def column(j):
        return jnp.concatenate([columns[j]] * repeats, axis=1)

    value = (row - column(0)) * column(DEG)
    for j in range(1, DEG):
        value = value * (row - column(j))
    return value


def split(value):
    high = value.astype(jnp.bfloat16)
    low = (value - high.astype(jnp.float32)).astype(jnp.bfloat16)
    return high, low


def paired_basis(basis_y, basis_z):
    return jnp.concatenate([basis_y[b : b + 1, :] * basis_z for b in range(NODES)], axis=0)


def up_kernel(count_ref, coords_ref, weights_ref, source_ref, target_ref, out_ref):
    basis = basis_columns(range(NODES))
    mixed = basis_columns(EVEN_ODD)
    lane = lax.broadcasted_iota(jnp.int32, (NODES, LANES), 1)
    row = lax.broadcasted_iota(jnp.int32, (NODES, LANES), 0)
    low_lanes = lane < PLANE

    def cluster(c):
        at = pl.ds(pl.multiple_of(c * PTS, PTS), PTS)
        basis_x = lagrange(coords_ref[0:1, at], mixed)
        basis_y = lagrange(coords_ref[1:2, at], basis)
        basis_z = lagrange(coords_ref[2:3, at], basis)
        left = jnp.concatenate([weights_ref[i : i + 1, at] * basis_x for i in range(3)], axis=0)
        left_rest = left - left.astype(jnp.bfloat16).astype(jnp.float32)
        left = jnp.concatenate([left, left_rest], axis=0).astype(jnp.bfloat16)
        right = jnp.concatenate(split(paired_basis(basis_y, basis_z)), axis=0)
        product = lax.dot_general(
            left, right, (((1,), (1,)), ((), ())), preferred_element_type=jnp.float32
        )
        both = product[: 3 * NODES] + product[3 * NODES :]
        return both + pltpu.roll(both, PLANE, 1)

    def pair(p, carry):
        first = cluster(2 * p)
        second = cluster(2 * p + 1)
        for i in range(3):
            one = first[i * NODES : (i + 1) * NODES]
            two = second[i * NODES : (i + 1) * NODES]
            one = jnp.where(low_lanes, one, pltpu.roll(one, 4, 0))
            two = jnp.where(low_lanes, pltpu.roll(two, 4, 0), two)
            at = pl.ds(pl.multiple_of(p * 24 + i * 8, 8), 8)
            out_ref[at, :] = jnp.where(row < 4, one, two)
        return carry

    lax.fori_loop(0, CL_DEV // 2, pair, 0)
    source = source_ref[...]
    target = target_ref[...]
    owner = lax.shift_right_logical(target, 4)
    payload = (source * CL_DEV + (target - owner * CL_DEV)).astype(jnp.float32)
    alive = lax.broadcasted_iota(jnp.int32, (1, TILES_DEV), 1) < count_ref[0]
    owner = jnp.where(alive, owner, -1).astype(jnp.float32)
    out_ref[CHARGE_ROWS:, :] = jnp.where(row == 0, payload, jnp.where(row == 1, owner, 0.0))


PIECES = (
    (0, 80, (1, 0, 2)),
    (80, 64, (2, 1, 0)),
    (144, 56, (0, 2, 1)),
)
ORDER = "010210210212"


def line_sizes():
    along_x = lax.axis_size("gx") // 2
    minor = lax.axis_size("gy")
    fast = max(n for n in range(1, minor + 1) if minor % n == 0 and n * n <= minor)
    return (along_x, minor // fast, fast)


def gather_kernel(sizes, offered_ref, out_ref, line_send, line_recv, core_send, core_recv, own_send, own_recv):
    major = lax.axis_index("gx")
    minor = lax.axis_index("gy")
    core = lax.rem(major, 2)
    at = (major // 2, minor // sizes[2], lax.rem(minor, sizes[2]))
    partner = (major + 1 - 2 * core, minor)

    def device(axis, by):
        spot = list(at)
        spot[axis] = spot[axis] + by
        return (spot[0] * 2 + core, spot[1] * sizes[2] + spot[2])

    steps = [[(axis, s) for axis in order for s in range(sizes[axis] - 1)] for _, _, order in PIECES]
    longest = max(len(s) for s in steps)

    def chunk(piece, step, j, of_core):
        first, count, order = PIECES[piece]
        axis = steps[piece][step][0]
        done = order[: order.index(axis)]
        spot = [slice(None) if n in done else (j if n == axis else at[n]) for n in range(3)]
        return out_ref.at[spot[0], of_core, spot[1], spot[2], pl.ds(first, count), :]

    def line_copy(piece, step, side, j):
        slot = (piece * longest + step) * 2 + (1 if side > 0 else 0)
        ref = chunk(piece, step, j, core)
        return pltpu.make_async_remote_copy(
            src_ref=ref,
            dst_ref=ref,
            send_sem=line_send.at[slot],
            recv_sem=line_recv.at[slot],
            device_id=device(steps[piece][step][0], side),
            device_id_type=pl.DeviceIdType.MESH,
        )

    def core_copy(piece, step, side, j, of_core):
        slot = (piece * longest + step) * 2 + (1 if side > 0 else 0)
        ref = chunk(piece, step, j, of_core)
        return pltpu.make_async_remote_copy(
            src_ref=ref,
            dst_ref=ref,
            send_sem=core_send.at[slot],
            recv_sem=core_recv.at[slot],
            device_id=partner,
            device_id_type=pl.DeviceIdType.MESH,
        )

    def own_copy(of_core):
        ref = out_ref.at[at[0], of_core, at[1], at[2]]
        return pltpu.make_async_remote_copy(
            src_ref=ref,
            dst_ref=ref,
            send_sem=own_send,
            recv_sem=own_recv,
            device_id=partner,
            device_id_type=pl.DeviceIdType.MESH,
        )

    def sends(piece, step, side):
        axis, s = steps[piece][step]
        j = at[axis] - side * s
        goes = (j >= 0) & (j < sizes[axis]) & (at[axis] + side >= 0) & (at[axis] + side < sizes[axis])
        return j, goes

    def arrives(piece, step, side):
        axis, s = steps[piece][step]
        j = at[axis] - side * (s + 1)
        return j, (j >= 0) & (j < sizes[axis])

    barrier = pltpu.get_barrier_semaphore()
    expected = jnp.int32(1)
    pl.semaphore_signal(barrier, inc=1, device_id=partner, device_id_type=pl.DeviceIdType.MESH)
    for axis in range(3):
        for side in (1, -1):
            there = (at[axis] + side >= 0) & (at[axis] + side < sizes[axis])
            expected = expected + there.astype(jnp.int32)

            @pl.when(there)
            def _(axis=axis, side=side):
                pl.semaphore_signal(
                    barrier, inc=1, device_id=device(axis, side), device_id_type=pl.DeviceIdType.MESH
                )

    out_ref[at[0], core, at[1], at[2]] = offered_ref[...]
    pl.semaphore_wait(barrier, expected)

    def start(piece, step):
        for side in (1, -1):
            j, goes = sends(piece, step, side)

            @pl.when(goes)
            def _(j=j, side=side):
                line_copy(piece, step, side, j).start()

    def receive(piece, step):
        for side in (1, -1):
            j, comes = arrives(piece, step, side)

            @pl.when(comes)
            def _(j=j, side=side):
                line_copy(piece, step, side, j).wait_recv()
                core_copy(piece, step, side, j, core).start()

    turns = [0, 1, 2] + [int(n) for n in ORDER]
    progress = [0] * len(PIECES)
    for piece in turns + [n for n in range(len(PIECES)) for _ in range(longest)]:
        step = progress[piece]
        if step > len(steps[piece]):
            continue
        if step > 0:
            receive(piece, step - 1)
        if step < len(steps[piece]):
            start(piece, step)
        progress[piece] = step + 1
        if step == 0 and piece == 2:
            own_copy(core).start()
    own_copy(core).wait_send()
    own_copy(1 - core).wait_recv()
    for piece in range(len(PIECES)):
        for step in range(len(steps[piece])):
            for side in (1, -1):
                j, goes = sends(piece, step, side)

                @pl.when(goes)
                def _(j=j, side=side, piece=piece, step=step):
                    line_copy(piece, step, side, j).wait_send()

                j, comes = arrives(piece, step, side)

                @pl.when(comes)
                def _(j=j, side=side, piece=piece, step=step):
                    core_copy(piece, step, side, j, core).wait_send()
                    core_copy(piece, step, side, j, 1 - core).wait_recv()


def gather(offered):
    sizes = line_sizes()
    slots = len(PIECES) * sum(n - 1 for n in sizes) * 2
    return pl.pallas_call(
        functools.partial(gather_kernel, sizes),
        out_shape=jax.ShapeDtypeStruct((sizes[0], 2, sizes[1], sizes[2], ROWS, LANES), jnp.float32),
        in_specs=[VMEM],
        out_specs=VMEM,
        scratch_shapes=[pltpu.SemaphoreType.DMA((slots,))] * 4 + [pltpu.SemaphoreType.DMA] * 2,
        compiler_params=pltpu.CompilerParams(
            collective_id=0, has_side_effects=True, vmem_limit_bytes=48 * 1024 * 1024
        ),
        name="gather",
    )(offered)


def table_kernel(capacity, me_ref, rows_ref, out_ref):
    domains = rows_ref.shape[0]
    rows = rows_ref[...]
    payload = jnp.concatenate([rows[d, 0:1, :] for d in range(domains)], axis=0)
    owner = jnp.concatenate([rows[d, 1:2, :] for d in range(domains)], axis=0)
    mine = owner == me_ref[0].astype(jnp.float32)
    before = lax.broadcasted_iota(jnp.int32, (TILES_DEV, TILES_DEV), 0)
    after = lax.broadcasted_iota(jnp.int32, (TILES_DEV, TILES_DEV), 1)
    earlier = (before < after).astype(jnp.float32).astype(jnp.bfloat16)
    rank = jnp.dot(
        mine.astype(jnp.float32).astype(jnp.bfloat16), earlier, preferred_element_type=jnp.float32
    )
    lane = lax.broadcasted_iota(jnp.int32, (domains, TILES_DEV), 1)
    table = jnp.full((domains, TILES_DEV), -1.0, jnp.float32)
    for r in range(capacity):
        chosen = jnp.where(mine & (rank == float(r)), payload + 1.0, 0.0)
        chosen = jnp.sum(chosen, axis=1, keepdims=True) - 1.0
        table = jnp.where(lane == r, chosen, table)
    out_ref[...] = table.astype(jnp.int32)


def tile_kernel(
    capacity,
    table_ref,
    centers_ref,
    widths_ref,
    charges_ref,
    coords_ref,
    lanes_ref,
    planes_ref,
    out_ref,
    list_ref,
    total_ref,
):
    domains = table_ref.shape[0]
    total_ref[...] = jnp.zeros_like(total_ref)

    def collect(d, found):
        for r in range(capacity):
            entry = table_ref[d, r]
            list_ref[found] = entry
            found = found + (entry >= 0).astype(jnp.int32)
        return found

    found = lax.fori_loop(0, domains, collect, jnp.int32(0))
    list_ref[found] = 0

    def tile(j):
        entry = list_ref[j]
        source = lax.shift_right_logical(entry, 4)
        local = lax.bitwise_and(entry, CL_DEV - 1)
        home = lax.shift_right_logical(source, 4)
        within = lax.bitwise_and(source, CL_DEV - 1)
        return entry, source, local, home, within

    def one_tile(j, me):
        _, source, local, home, within = tile(j)
        target = me * CL_DEV + local
        scale = jnp.where(j < found, jnp.float32(biot_factor), jnp.float32(0.0))
        width_t = widths_ref[target]
        width_s = widths_ref[source]
        shift = [centers_ref[i, target] - centers_ref[i, source] for i in range(3)]
        first_row = lax.shift_right_logical(within, 1) * 24 + lax.bitwise_and(within, 1) * 4
        charge = [
            jnp.concatenate(
                [charges_ref[home, pl.ds(first_row + i * 8 + g, 1), :] for g in range(GROUPS)], axis=1
            )
            for i in range(3)
        ]
        unit = [lanes_ref[i : i + 1, :] for i in range(3)]
        near = [width_s * unit[i] for i in range(3)]
        moment = [
            near[1] * charge[2] - near[2] * charge[1],
            near[2] * charge[0] - near[0] * charge[2],
            near[0] * charge[1] - near[1] * charge[0],
        ]
        nothing = jnp.zeros((2, PROXIES), jnp.float32)
        features = jnp.concatenate(charge + moment + [nothing], axis=0)
        rest = features - features.astype(jnp.bfloat16).astype(jnp.float32)
        features = jnp.concatenate([features, rest], axis=0).astype(jnp.bfloat16)
        place = [width_t * unit[i] + shift[i] for i in range(3)]
        along_x = place[0] - width_s * lanes_ref[8:16, :]
        along_x = along_x * along_x
        along_y = place[1][:, :LANES] - width_s * planes_ref[:, :LANES]
        along_z = place[2][:, :LANES] - width_s * planes_ref[:, LANES:]
        plane = along_y * along_y + along_z * along_z + smoothing_sq
        summed = jnp.zeros((16, PROXIES), jnp.float32)
        for half in range(2):
            blocks = []
            for a in range(half * 4, half * 4 + 4):
                radius_sq = jnp.concatenate(
                    [plane + along_x[a : a + 1, g * LANES : (g + 1) * LANES] for g in range(GROUPS)], axis=1
                )
                inverse = lax.rsqrt(radius_sq)
                blocks.append(inverse * inverse * inverse)
            high, low = split(jnp.concatenate(blocks, axis=0))
            part = features[:, half * 256 : (half + 1) * 256]
            summed = summed + jnp.dot(part, high, preferred_element_type=jnp.float32)
            summed = summed + jnp.dot(part, low, preferred_element_type=jnp.float32)
        both = (summed[:8] + summed[8:]) * scale
        s = [both[i : i + 1] for i in range(6)]
        velocity = [
            place[1] * s[2] - place[2] * s[1] - s[3],
            place[2] * s[0] - place[0] * s[2] - s[4],
            place[0] * s[1] - place[1] * s[0] - s[5],
        ]
        return local, velocity

    me = lax.axis_index(AXES)

    def two_tiles(i, carry):
        for local, velocity in [one_tile(2 * i, me), one_tile(2 * i + 1, me)]:
            for n in range(3):
                total_ref[local, n : n + 1, :] += velocity[n]
        return carry

    lax.fori_loop(0, lax.shift_right_logical(found + 1, 1), two_tiles, 0)

    basis = basis_columns(range(NODES))

    def down(c, carry):
        at = pl.ds(pl.multiple_of(c * PTS, PTS), PTS)
        basis_x = lagrange(coords_ref[0:1, at], basis)
        basis_y = lagrange(coords_ref[1:2, at], basis)
        basis_z = lagrange(coords_ref[2:3, at], basis)
        high, low = split(paired_basis(basis_y, basis_z))
        values = total_ref[c]
        values = jnp.concatenate([values[:, a * PLANE : (a + 1) * PLANE] for a in range(NODES)], axis=0)
        values_high, values_low = split(values)
        spread = jnp.dot(values_high, high, preferred_element_type=jnp.float32)
        spread = spread + jnp.dot(values_low, high, preferred_element_type=jnp.float32)
        spread = spread + jnp.dot(values_high, low, preferred_element_type=jnp.float32)
        velocity = basis_x[0:1, :] * spread[0:8]
        for a in range(1, NODES):
            velocity = velocity + basis_x[a : a + 1, :] * spread[a * 8 : (a + 1) * 8]
        out_ref[:, at] = velocity[:3]
        return carry

    lax.fori_loop(0, CL_DEV, down, 0)


def local(point_coords, strengths, centers, half_widths, tile_source, tile_target, tile_count):
    domains = lax.axis_size(AXES)
    capacity = (TILES_DEV + domains - 1) // domains
    params = pltpu.CompilerParams(vmem_limit_bytes=48 * 1024 * 1024)

    def whole(*shape):
        return pl.BlockSpec(shape, lambda i: (0,) * len(shape))

    offered = pl.pallas_call(
        up_kernel,
        grid=(1,),
        out_shape=jax.ShapeDtypeStruct((ROWS, LANES), jnp.float32),
        in_specs=[SMEM]
        + [whole(3, CL_DEV * PTS), whole(3, CL_DEV * PTS), whole(1, TILES_DEV), whole(1, TILES_DEV)],
        out_specs=whole(ROWS, LANES),
        compiler_params=params,
        name="upward",
    )(tile_count, point_coords, strengths, tile_source, tile_target)
    gathered = gather(offered).reshape(domains, ROWS, LANES)
    me = lax.axis_index(AXES).astype(jnp.int32).reshape(1)
    table = pl.pallas_call(
        functools.partial(table_kernel, capacity),
        grid=(1,),
        out_shape=jax.ShapeDtypeStruct((domains, TILES_DEV), jnp.int32),
        in_specs=[SMEM, pl.BlockSpec((domains, 8, LANES), lambda i: (0, CHARGE_ROWS // 8, 0))],
        out_specs=pl.BlockSpec((domains, TILES_DEV), lambda i: (0, 0)),
        compiler_params=params,
        name="tables",
    )(me, gathered)
    return pl.pallas_call(
        functools.partial(tile_kernel, capacity),
        out_shape=jax.ShapeDtypeStruct((3, CL_DEV * PTS), jnp.float32),
        in_specs=[SMEM] * 3 + [VMEM] * 4,
        out_specs=VMEM,
        scratch_shapes=[
            pltpu.SMEM((domains * capacity + 8,), jnp.int32),
            pltpu.VMEM((CL_DEV, 8, PROXIES), jnp.float32),
        ],
        compiler_params=params,
        name="tiles",
    )(
        table,
        centers,
        half_widths,
        gathered,
        point_coords,
        jnp.asarray(lane_tables()),
        jnp.asarray(plane_tables()),
    )


def solution(mesh):
    return jax.shard_map(
        local,
        mesh=mesh,
        in_specs=(
            P(None, AXES),
            P(None, AXES),
            P(),
            P(),
            P(AXES, None),
            P(AXES, None),
            P(AXES),
        ),
        out_specs=P(None, AXES),
        check_vma=False,
    )
```

```python
import functools

import jax
import jax.numpy as jnp
import numpy as np
from jax import lax
from jax.experimental import pallas as pl
from jax.experimental.pallas import tpu as pltpu
from jax.sharding import PartitionSpec as P

CL_DEV = 16
PTS = 1024
DEG = 7
TILES_DEV = 128
AXES = ("gx", "gy")

NODES = DEG + 1
PLANE = NODES * NODES
PROXIES = NODES**3
LANES = 128
GROUPS = PROXIES // LANES
CHARGE_ROWS = CL_DEV * 3 * GROUPS
ROWS = CHARGE_ROWS + 8
smoothing_sq = 0.01
biot_factor = -0.07957747154594767

CHEB = np.cos(np.pi * np.arange(NODES) / DEG)
EVEN_ODD = [0, 2, 4, 6, 1, 3, 5, 7]
VMEM = pl.BlockSpec(memory_space=pltpu.VMEM)
SMEM = pl.BlockSpec(memory_space=pltpu.SMEM)


def basis_columns(order):
    row = lax.broadcasted_iota(jnp.int32, (NODES, LANES), 0)

    def column(values):
        tile = jnp.full((NODES, LANES), float(values[0]), jnp.float32)
        for n in range(1, NODES):
            tile = jnp.where(row == n, jnp.float32(values[n]), tile)
        return tile

    others = [[m for m in range(NODES) if m != a] for a in order]
    columns = [column([CHEB[left[j]] for left in others]) for j in range(DEG)]
    inverse = [1.0 / np.prod([CHEB[a] - CHEB[m] for m in left]) for a, left in zip(order, others)]
    return columns + [column(inverse)]


def lane_tables():
    k = np.arange(PROXIES)
    table = np.zeros((16, PROXIES), np.float32)
    table[0] = CHEB[k // PLANE]
    table[1] = CHEB[(k // NODES) % NODES]
    table[2] = CHEB[k % NODES]
    table[8:16] = CHEB[:, None]
    return table


def plane_tables():
    rows = np.arange(PLANE)
    along_y = np.repeat(CHEB[rows // NODES][:, None], LANES, axis=1)
    along_z = np.repeat(CHEB[rows % NODES][:, None], LANES, axis=1)
    return np.concatenate([along_y, along_z], axis=1).astype(np.float32)


def lagrange(row, columns):
    repeats = row.shape[1] // LANES

    def column(j):
        return jnp.concatenate([columns[j]] * repeats, axis=1)

    value = (row - column(0)) * column(DEG)
    for j in range(1, DEG):
        value = value * (row - column(j))
    return value


def split(value):
    high = value.astype(jnp.bfloat16)
    low = (value - high.astype(jnp.float32)).astype(jnp.bfloat16)
    return high, low


def paired_basis(basis_y, basis_z):
    return jnp.concatenate([basis_y[b : b + 1, :] * basis_z for b in range(NODES)], axis=0)


def up_kernel(count_ref, coords_ref, weights_ref, source_ref, target_ref, out_ref):
    basis = basis_columns(range(NODES))
    mixed = basis_columns(EVEN_ODD)
    lane = lax.broadcasted_iota(jnp.int32, (NODES, LANES), 1)
    row = lax.broadcasted_iota(jnp.int32, (NODES, LANES), 0)
    low_lanes = lane < PLANE

    def cluster(c):
        at = pl.ds(pl.multiple_of(c * PTS, PTS), PTS)
        basis_x = lagrange(coords_ref[0:1, at], mixed)
        basis_y = lagrange(coords_ref[1:2, at], basis)
        basis_z = lagrange(coords_ref[2:3, at], basis)
        left = jnp.concatenate([weights_ref[i : i + 1, at] * basis_x for i in range(3)], axis=0)
        left_rest = left - left.astype(jnp.bfloat16).astype(jnp.float32)
        left = jnp.concatenate([left, left_rest], axis=0).astype(jnp.bfloat16)
        right = jnp.concatenate(split(paired_basis(basis_y, basis_z)), axis=0)
        product = lax.dot_general(
            left, right, (((1,), (1,)), ((), ())), preferred_element_type=jnp.float32
        )
        both = product[: 3 * NODES] + product[3 * NODES :]
        return both + pltpu.roll(both, PLANE, 1)

    def pair(p, carry):
        first = cluster(2 * p)
        second = cluster(2 * p + 1)
        for i in range(3):
            one = first[i * NODES : (i + 1) * NODES]
            two = second[i * NODES : (i + 1) * NODES]
            one = jnp.where(low_lanes, one, pltpu.roll(one, 4, 0))
            two = jnp.where(low_lanes, pltpu.roll(two, 4, 0), two)
            at = pl.ds(pl.multiple_of(p * 24 + i * 8, 8), 8)
            out_ref[at, :] = jnp.where(row < 4, one, two)
        return carry

    lax.fori_loop(0, CL_DEV // 2, pair, 0)
    source = source_ref[...]
    target = target_ref[...]
    owner = lax.shift_right_logical(target, 4)
    payload = (source * CL_DEV + (target - owner * CL_DEV)).astype(jnp.float32)
    alive = lax.broadcasted_iota(jnp.int32, (1, TILES_DEV), 1) < count_ref[0]
    owner = jnp.where(alive, owner, -1).astype(jnp.float32)
    out_ref[CHARGE_ROWS:, :] = jnp.where(row == 0, payload, jnp.where(row == 1, owner, 0.0))


PIECES = (
    (0, 80, (1, 0, 2)),
    (80, 64, (2, 1, 0)),
    (144, 56, (0, 2, 1)),
)
ORDER = "010210210212"


def line_sizes():
    along_x = lax.axis_size("gx") // 2
    minor = lax.axis_size("gy")
    fast = max(n for n in range(1, minor + 1) if minor % n == 0 and n * n <= minor)
    return (along_x, minor // fast, fast)


def gather_kernel(sizes, offered_ref, out_ref, line_send, line_recv, core_send, core_recv, own_send, own_recv):
    major = lax.axis_index("gx")
    minor = lax.axis_index("gy")
    core = lax.rem(major, 2)
    at = (major // 2, minor // sizes[2], lax.rem(minor, sizes[2]))
    partner = (major + 1 - 2 * core, minor)

    def device(axis, by):
        spot = list(at)
        spot[axis] = spot[axis] + by
        return (spot[0] * 2 + core, spot[1] * sizes[2] + spot[2])

    steps = [[(axis, s) for axis in order for s in range(sizes[axis] - 1)] for _, _, order in PIECES]
    longest = max(len(s) for s in steps)

    def chunk(piece, step, j, of_core):
        first, count, order = PIECES[piece]
        axis = steps[piece][step][0]
        done = order[: order.index(axis)]
        spot = [slice(None) if n in done else (j if n == axis else at[n]) for n in range(3)]
        return out_ref.at[spot[0], of_core, spot[1], spot[2], pl.ds(first, count), :]

    def line_copy(piece, step, side, j):
        slot = (piece * longest + step) * 2 + (1 if side > 0 else 0)
        ref = chunk(piece, step, j, core)
        return pltpu.make_async_remote_copy(
            src_ref=ref,
            dst_ref=ref,
            send_sem=line_send.at[slot],
            recv_sem=line_recv.at[slot],
            device_id=device(steps[piece][step][0], side),
            device_id_type=pl.DeviceIdType.MESH,
        )

    def core_copy(piece, step, side, j, of_core):
        slot = (piece * longest + step) * 2 + (1 if side > 0 else 0)
        ref = chunk(piece, step, j, of_core)
        return pltpu.make_async_remote_copy(
            src_ref=ref,
            dst_ref=ref,
            send_sem=core_send.at[slot],
            recv_sem=core_recv.at[slot],
            device_id=partner,
            device_id_type=pl.DeviceIdType.MESH,
        )

    def own_copy(of_core):
        ref = out_ref.at[at[0], of_core, at[1], at[2]]
        return pltpu.make_async_remote_copy(
            src_ref=ref,
            dst_ref=ref,
            send_sem=own_send,
            recv_sem=own_recv,
            device_id=partner,
            device_id_type=pl.DeviceIdType.MESH,
        )

    def sends(piece, step, side):
        axis, s = steps[piece][step]
        j = at[axis] - side * s
        goes = (j >= 0) & (j < sizes[axis]) & (at[axis] + side >= 0) & (at[axis] + side < sizes[axis])
        return j, goes

    def arrives(piece, step, side):
        axis, s = steps[piece][step]
        j = at[axis] - side * (s + 1)
        return j, (j >= 0) & (j < sizes[axis])

    barrier = pltpu.get_barrier_semaphore()
    expected = jnp.int32(1)
    pl.semaphore_signal(barrier, inc=1, device_id=partner, device_id_type=pl.DeviceIdType.MESH)
    for axis in range(3):
        for side in (1, -1):
            there = (at[axis] + side >= 0) & (at[axis] + side < sizes[axis])
            expected = expected + there.astype(jnp.int32)

            @pl.when(there)
            def _(axis=axis, side=side):
                pl.semaphore_signal(
                    barrier, inc=1, device_id=device(axis, side), device_id_type=pl.DeviceIdType.MESH
                )

    out_ref[at[0], core, at[1], at[2]] = offered_ref[...]
    pl.semaphore_wait(barrier, expected)

    def start(piece, step):
        for side in (1, -1):
            j, goes = sends(piece, step, side)

            @pl.when(goes)
            def _(j=j, side=side):
                line_copy(piece, step, side, j).start()

    def receive(piece, step):
        for side in (1, -1):
            j, comes = arrives(piece, step, side)

            @pl.when(comes)
            def _(j=j, side=side):
                line_copy(piece, step, side, j).wait_recv()
                core_copy(piece, step, side, j, core).start()

    turns = [0, 1, 2] + [int(n) for n in ORDER]
    progress = [0] * len(PIECES)
    for piece in turns + [n for n in range(len(PIECES)) for _ in range(longest)]:
        step = progress[piece]
        if step > len(steps[piece]):
            continue
        if step > 0:
            receive(piece, step - 1)
        if step < len(steps[piece]):
            start(piece, step)
        progress[piece] = step + 1
        if step == 0 and piece == 2:
            own_copy(core).start()
    own_copy(core).wait_send()
    own_copy(1 - core).wait_recv()
    for piece in range(len(PIECES)):
        for step in range(len(steps[piece])):
            for side in (1, -1):
                j, goes = sends(piece, step, side)

                @pl.when(goes)
                def _(j=j, side=side, piece=piece, step=step):
                    line_copy(piece, step, side, j).wait_send()

                j, comes = arrives(piece, step, side)

                @pl.when(comes)
                def _(j=j, side=side, piece=piece, step=step):
                    core_copy(piece, step, side, j, core).wait_send()
                    core_copy(piece, step, side, j, 1 - core).wait_recv()


def gather(offered):
    sizes = line_sizes()
    slots = len(PIECES) * sum(n - 1 for n in sizes) * 2
    return pl.pallas_call(
        functools.partial(gather_kernel, sizes),
        out_shape=jax.ShapeDtypeStruct((sizes[0], 2, sizes[1], sizes[2], ROWS, LANES), jnp.float32),
        in_specs=[VMEM],
        out_specs=VMEM,
        scratch_shapes=[pltpu.SemaphoreType.DMA((slots,))] * 4 + [pltpu.SemaphoreType.DMA] * 2,
        compiler_params=pltpu.CompilerParams(
            collective_id=0, has_side_effects=True, vmem_limit_bytes=48 * 1024 * 1024
        ),
        name="gather",
    )(offered)


def table_kernel(capacity, me_ref, rows_ref, out_ref):
    domains = rows_ref.shape[0]
    rows = rows_ref[...]
    payload = jnp.concatenate([rows[d, 0:1, :] for d in range(domains)], axis=0)
    owner = jnp.concatenate([rows[d, 1:2, :] for d in range(domains)], axis=0)
    mine = owner == me_ref[0].astype(jnp.float32)
    before = lax.broadcasted_iota(jnp.int32, (TILES_DEV, TILES_DEV), 0)
    after = lax.broadcasted_iota(jnp.int32, (TILES_DEV, TILES_DEV), 1)
    earlier = (before < after).astype(jnp.float32).astype(jnp.bfloat16)
    rank = jnp.dot(
        mine.astype(jnp.float32).astype(jnp.bfloat16), earlier, preferred_element_type=jnp.float32
    )
    lane = lax.broadcasted_iota(jnp.int32, (domains, TILES_DEV), 1)
    table = jnp.full((domains, TILES_DEV), -1.0, jnp.float32)
    for r in range(capacity):
        chosen = jnp.where(mine & (rank == float(r)), payload + 1.0, 0.0)
        chosen = jnp.sum(chosen, axis=1, keepdims=True) - 1.0
        table = jnp.where(lane == r, chosen, table)
    out_ref[...] = table.astype(jnp.int32)


def tile_kernel(
    capacity,
    table_ref,
    centers_ref,
    widths_ref,
    charges_ref,
    coords_ref,
    lanes_ref,
    planes_ref,
    out_ref,
    list_ref,
    total_ref,
    matrix_ref,
):
    domains = table_ref.shape[0]
    total_ref[...] = jnp.zeros_like(total_ref)

    def collect(d, found):
        for r in range(capacity):
            entry = table_ref[d, r]
            list_ref[found] = entry
            found = found + (entry >= 0).astype(jnp.int32)
        return found

    found = lax.fori_loop(0, domains, collect, jnp.int32(0))
    list_ref[found] = 0

    def tile(j):
        entry = list_ref[j]
        source = lax.shift_right_logical(entry, 4)
        local = lax.bitwise_and(entry, CL_DEV - 1)
        home = lax.shift_right_logical(source, 4)
        within = lax.bitwise_and(source, CL_DEV - 1)
        return entry, source, local, home, within

    def one_tile(j, me, slot):
        _, source, local, home, within = tile(j)
        target = me * CL_DEV + local
        scale = jnp.where(j < found, jnp.float32(biot_factor), jnp.float32(0.0))
        width_t = widths_ref[target]
        width_s = widths_ref[source]
        shift = [centers_ref[i, target] - centers_ref[i, source] for i in range(3)]
        first_row = lax.shift_right_logical(within, 1) * 24 + lax.bitwise_and(within, 1) * 4
        charge = [
            jnp.concatenate(
                [charges_ref[home, pl.ds(first_row + i * 8 + g, 1), :] for g in range(GROUPS)], axis=1
            )
            for i in range(3)
        ]
        unit = [lanes_ref[i : i + 1, :] for i in range(3)]
        near = [width_s * unit[i] for i in range(3)]
        moment = [
            near[1] * charge[2] - near[2] * charge[1],
            near[2] * charge[0] - near[0] * charge[2],
            near[0] * charge[1] - near[1] * charge[0],
        ]
        nothing = jnp.zeros((2, PROXIES), jnp.float32)
        features = jnp.concatenate(charge + moment + [nothing], axis=0)
        rest = features - features.astype(jnp.bfloat16).astype(jnp.float32)
        features = jnp.concatenate([features, rest], axis=0).astype(jnp.bfloat16)
        place = [width_t * unit[i] + shift[i] for i in range(3)]
        along_x = place[0] - width_s * lanes_ref[8:16, :]
        along_x = along_x * along_x
        along_y = place[1][:, :LANES] - width_s * planes_ref[:, :LANES]
        along_z = place[2][:, :LANES] - width_s * planes_ref[:, LANES:]
        plane = along_y * along_y + along_z * along_z + smoothing_sq
        summed = None
        for half in range(2):
            for n in range(4):
                a = half * 4 + n
                for g in range(GROUPS):
                    lanes = slice(g * LANES, (g + 1) * LANES)
                    inverse = lax.rsqrt(plane + along_x[a : a + 1, lanes])
                    high, low = split(inverse * inverse * inverse)
                    matrix_ref[slot, half, n * PLANE : (n + 1) * PLANE, lanes] = high
                    matrix_ref[slot, half, (4 + n) * PLANE : (5 + n) * PLANE, lanes] = low
            part = features[:, half * 256 : (half + 1) * 256]
            part = jnp.concatenate([part, part], axis=1)
            product = jnp.dot(part, matrix_ref[slot, half], preferred_element_type=jnp.float32)
            summed = product if summed is None else summed + product
        both = (summed[:8] + summed[8:]) * scale
        s = [both[i : i + 1] for i in range(6)]
        velocity = [
            place[1] * s[2] - place[2] * s[1] - s[3],
            place[2] * s[0] - place[0] * s[2] - s[4],
            place[0] * s[1] - place[1] * s[0] - s[5],
        ]
        return local, velocity

    me = lax.axis_index(AXES)

    def two_tiles(i, carry):
        for local, velocity in [one_tile(2 * i, me, 0), one_tile(2 * i + 1, me, 1)]:
            for n in range(3):
                total_ref[local, n : n + 1, :] += velocity[n]
        return carry

    lax.fori_loop(0, lax.shift_right_logical(found + 1, 1), two_tiles, 0)

    basis = basis_columns(range(NODES))

    def down(c, carry):
        at = pl.ds(pl.multiple_of(c * PTS, PTS), PTS)
        basis_x = lagrange(coords_ref[0:1, at], basis)
        basis_y = lagrange(coords_ref[1:2, at], basis)
        basis_z = lagrange(coords_ref[2:3, at], basis)
        high, low = split(paired_basis(basis_y, basis_z))
        values = total_ref[c]
        values = jnp.concatenate([values[:, a * PLANE : (a + 1) * PLANE] for a in range(NODES)], axis=0)
        values_high, values_low = split(values)
        spread = jnp.dot(values_high, high, preferred_element_type=jnp.float32)
        spread = spread + jnp.dot(values_low, high, preferred_element_type=jnp.float32)
        spread = spread + jnp.dot(values_high, low, preferred_element_type=jnp.float32)
        velocity = basis_x[0:1, :] * spread[0:8]
        for a in range(1, NODES):
            velocity = velocity + basis_x[a : a + 1, :] * spread[a * 8 : (a + 1) * 8]
        out_ref[:, at] = velocity[:3]
        return carry

    lax.fori_loop(0, CL_DEV, down, 0)


def local(point_coords, strengths, centers, half_widths, tile_source, tile_target, tile_count):
    domains = lax.axis_size(AXES)
    capacity = (TILES_DEV + domains - 1) // domains
    params = pltpu.CompilerParams(vmem_limit_bytes=48 * 1024 * 1024)

    def whole(*shape):
        return pl.BlockSpec(shape, lambda i: (0,) * len(shape))

    offered = pl.pallas_call(
        up_kernel,
        grid=(1,),
        out_shape=jax.ShapeDtypeStruct((ROWS, LANES), jnp.float32),
        in_specs=[SMEM]
        + [whole(3, CL_DEV * PTS), whole(3, CL_DEV * PTS), whole(1, TILES_DEV), whole(1, TILES_DEV)],
        out_specs=whole(ROWS, LANES),
        compiler_params=params,
        name="upward",
    )(tile_count, point_coords, strengths, tile_source, tile_target)
    gathered = gather(offered).reshape(domains, ROWS, LANES)
    me = lax.axis_index(AXES).astype(jnp.int32).reshape(1)
    table = pl.pallas_call(
        functools.partial(table_kernel, capacity),
        grid=(1,),
        out_shape=jax.ShapeDtypeStruct((domains, TILES_DEV), jnp.int32),
        in_specs=[SMEM, pl.BlockSpec((domains, 8, LANES), lambda i: (0, CHARGE_ROWS // 8, 0))],
        out_specs=pl.BlockSpec((domains, TILES_DEV), lambda i: (0, 0)),
        compiler_params=params,
        name="tables",
    )(me, gathered)
    return pl.pallas_call(
        functools.partial(tile_kernel, capacity),
        out_shape=jax.ShapeDtypeStruct((3, CL_DEV * PTS), jnp.float32),
        in_specs=[SMEM] * 3 + [VMEM] * 4,
        out_specs=VMEM,
        scratch_shapes=[
            pltpu.SMEM((domains * capacity + 8,), jnp.int32),
            pltpu.VMEM((CL_DEV, 8, PROXIES), jnp.float32),
            pltpu.VMEM((2, 2, PROXIES, PROXIES), jnp.bfloat16),
        ],
        compiler_params=params,
        name="tiles",
    )(
        table,
        centers,
        half_widths,
        gathered,
        point_coords,
        jnp.asarray(lane_tables()),
        jnp.asarray(plane_tables()),
    )


def solution(mesh):
    return jax.shard_map(
        local,
        mesh=mesh,
        in_specs=(
            P(None, AXES),
            P(None, AXES),
            P(),
            P(),
            P(AXES, None),
            P(AXES, None),
            P(AXES),
        ),
        out_specs=P(None, AXES),
        check_vma=False,
    )
```

```python
import functools

import jax
import jax.numpy as jnp
import numpy as np
from jax import lax
from jax.experimental import pallas as pl
from jax.experimental.pallas import tpu as pltpu
from jax.sharding import PartitionSpec as P

CL_DEV = 16
PTS = 1024
DEG = 7
TILES_DEV = 128
AXES = ("gx", "gy")

NODES = DEG + 1
PLANE = NODES * NODES
PROXIES = NODES**3
LANES = 128
GROUPS = PROXIES // LANES
CHARGE_ROWS = CL_DEV * 3 * GROUPS
ROWS = CHARGE_ROWS + 8
smoothing_sq = 0.01
biot_factor = -0.07957747154594767

CHEB = np.cos(np.pi * np.arange(NODES) / DEG)
EVEN_ODD = [0, 2, 4, 6, 1, 3, 5, 7]
VMEM = pl.BlockSpec(memory_space=pltpu.VMEM)
SMEM = pl.BlockSpec(memory_space=pltpu.SMEM)


def basis_columns(order):
    row = lax.broadcasted_iota(jnp.int32, (NODES, LANES), 0)

    def column(values):
        tile = jnp.full((NODES, LANES), float(values[0]), jnp.float32)
        for n in range(1, NODES):
            tile = jnp.where(row == n, jnp.float32(values[n]), tile)
        return tile

    others = [[m for m in range(NODES) if m != a] for a in order]
    columns = [column([CHEB[left[j]] for left in others]) for j in range(DEG)]
    inverse = [1.0 / np.prod([CHEB[a] - CHEB[m] for m in left]) for a, left in zip(order, others)]
    return columns + [column(inverse)]


def lane_tables():
    k = np.arange(PROXIES)
    table = np.zeros((16, PROXIES), np.float32)
    table[0] = CHEB[k // PLANE]
    table[1] = CHEB[(k // NODES) % NODES]
    table[2] = CHEB[k % NODES]
    table[8:16] = CHEB[:, None]
    return table


def plane_tables():
    rows = np.arange(PLANE)
    along_y = np.repeat(CHEB[rows // NODES][:, None], LANES, axis=1)
    along_z = np.repeat(CHEB[rows % NODES][:, None], LANES, axis=1)
    return np.concatenate([along_y, along_z], axis=1).astype(np.float32)


def lagrange(row, columns):
    repeats = row.shape[1] // LANES

    def column(j):
        return jnp.concatenate([columns[j]] * repeats, axis=1)

    value = (row - column(0)) * column(DEG)
    for j in range(1, DEG):
        value = value * (row - column(j))
    return value


def split(value):
    high = value.astype(jnp.bfloat16)
    low = (value - high.astype(jnp.float32)).astype(jnp.bfloat16)
    return high, low


def paired_basis(basis_y, basis_z):
    return jnp.concatenate([basis_y[b : b + 1, :] * basis_z for b in range(NODES)], axis=0)


def up_kernel(count_ref, coords_ref, weights_ref, source_ref, target_ref, out_ref):
    basis = basis_columns(range(NODES))
    mixed = basis_columns(EVEN_ODD)
    lane = lax.broadcasted_iota(jnp.int32, (NODES, LANES), 1)
    row = lax.broadcasted_iota(jnp.int32, (NODES, LANES), 0)
    low_lanes = lane < PLANE

    def cluster(c):
        at = pl.ds(pl.multiple_of(c * PTS, PTS), PTS)
        basis_x = lagrange(coords_ref[0:1, at], mixed)
        basis_y = lagrange(coords_ref[1:2, at], basis)
        basis_z = lagrange(coords_ref[2:3, at], basis)
        left = jnp.concatenate([weights_ref[i : i + 1, at] * basis_x for i in range(3)], axis=0)
        left_rest = left - left.astype(jnp.bfloat16).astype(jnp.float32)
        left = jnp.concatenate([left, left_rest], axis=0).astype(jnp.bfloat16)
        right = jnp.concatenate(split(paired_basis(basis_y, basis_z)), axis=0)
        product = lax.dot_general(
            left, right, (((1,), (1,)), ((), ())), preferred_element_type=jnp.float32
        )
        both = product[: 3 * NODES] + product[3 * NODES :]
        return both + pltpu.roll(both, PLANE, 1)

    def pair(p, carry):
        first = cluster(2 * p)
        second = cluster(2 * p + 1)
        for i in range(3):
            one = first[i * NODES : (i + 1) * NODES]
            two = second[i * NODES : (i + 1) * NODES]
            one = jnp.where(low_lanes, one, pltpu.roll(one, 4, 0))
            two = jnp.where(low_lanes, pltpu.roll(two, 4, 0), two)
            at = pl.ds(pl.multiple_of(p * 24 + i * 8, 8), 8)
            out_ref[at, :] = jnp.where(row < 4, one, two)
        return carry

    lax.fori_loop(0, CL_DEV // 2, pair, 0)
    source = source_ref[...]
    target = target_ref[...]
    owner = lax.shift_right_logical(target, 4)
    payload = (source * CL_DEV + (target - owner * CL_DEV)).astype(jnp.float32)
    alive = lax.broadcasted_iota(jnp.int32, (1, TILES_DEV), 1) < count_ref[0]
    owner = jnp.where(alive, owner, -1).astype(jnp.float32)
    out_ref[CHARGE_ROWS:, :] = jnp.where(row == 0, payload, jnp.where(row == 1, owner, 0.0))


PIECES = (
    (0, 40, (1, 0, 2)),
    (40, 48, (1, 0, 2)),
    (88, 32, (2, 1, 0)),
    (120, 40, (2, 1, 0)),
    (160, 40, (0, 2, 1)),
)
ORDER = "01021042312034213434"


def line_sizes():
    along_x = lax.axis_size("gx") // 2
    minor = lax.axis_size("gy")
    fast = max(n for n in range(1, minor + 1) if minor % n == 0 and n * n <= minor)
    return (along_x, minor // fast, fast)


def gather_kernel(sizes, offered_ref, out_ref, line_send, line_recv, core_send, core_recv, own_send, own_recv):
    major = lax.axis_index("gx")
    minor = lax.axis_index("gy")
    core = lax.rem(major, 2)
    at = (major // 2, minor // sizes[2], lax.rem(minor, sizes[2]))
    partner = (major + 1 - 2 * core, minor)

    def device(axis, by):
        spot = list(at)
        spot[axis] = spot[axis] + by
        return (spot[0] * 2 + core, spot[1] * sizes[2] + spot[2])

    steps = [[(axis, s) for axis in order for s in range(sizes[axis] - 1)] for _, _, order in PIECES]
    longest = max(len(s) for s in steps)

    def chunk(piece, step, j, of_core):
        first, count, order = PIECES[piece]
        axis = steps[piece][step][0]
        done = order[: order.index(axis)]
        spot = [slice(None) if n in done else (j if n == axis else at[n]) for n in range(3)]
        return out_ref.at[spot[0], of_core, spot[1], spot[2], pl.ds(first, count), :]

    def line_copy(piece, step, side, j):
        slot = (piece * longest + step) * 2 + (1 if side > 0 else 0)
        ref = chunk(piece, step, j, core)
        return pltpu.make_async_remote_copy(
            src_ref=ref,
            dst_ref=ref,
            send_sem=line_send.at[slot],
            recv_sem=line_recv.at[slot],
            device_id=device(steps[piece][step][0], side),
            device_id_type=pl.DeviceIdType.MESH,
        )

    def core_copy(piece, step, side, j, of_core):
        slot = (piece * longest + step) * 2 + (1 if side > 0 else 0)
        ref = chunk(piece, step, j, of_core)
        return pltpu.make_async_remote_copy(
            src_ref=ref,
            dst_ref=ref,
            send_sem=core_send.at[slot],
            recv_sem=core_recv.at[slot],
            device_id=partner,
            device_id_type=pl.DeviceIdType.MESH,
        )

    def own_copy(of_core):
        ref = out_ref.at[at[0], of_core, at[1], at[2]]
        return pltpu.make_async_remote_copy(
            src_ref=ref,
            dst_ref=ref,
            send_sem=own_send,
            recv_sem=own_recv,
            device_id=partner,
            device_id_type=pl.DeviceIdType.MESH,
        )

    def sends(piece, step, side):
        axis, s = steps[piece][step]
        j = at[axis] - side * s
        goes = (j >= 0) & (j < sizes[axis]) & (at[axis] + side >= 0) & (at[axis] + side < sizes[axis])
        return j, goes

    def arrives(piece, step, side):
        axis, s = steps[piece][step]
        j = at[axis] - side * (s + 1)
        return j, (j >= 0) & (j < sizes[axis])

    barrier = pltpu.get_barrier_semaphore()
    expected = jnp.int32(1)
    pl.semaphore_signal(barrier, inc=1, device_id=partner, device_id_type=pl.DeviceIdType.MESH)
    for axis in range(3):
        for side in (1, -1):
            there = (at[axis] + side >= 0) & (at[axis] + side < sizes[axis])
            expected = expected + there.astype(jnp.int32)

            @pl.when(there)
            def _(axis=axis, side=side):
                pl.semaphore_signal(
                    barrier, inc=1, device_id=device(axis, side), device_id_type=pl.DeviceIdType.MESH
                )

    out_ref[at[0], core, at[1], at[2]] = offered_ref[...]
    pl.semaphore_wait(barrier, expected)

    def start(piece, step):
        for side in (1, -1):
            j, goes = sends(piece, step, side)

            @pl.when(goes)
            def _(j=j, side=side):
                line_copy(piece, step, side, j).start()

    def receive(piece, step):
        for side in (1, -1):
            j, comes = arrives(piece, step, side)

            @pl.when(comes)
            def _(j=j, side=side):
                line_copy(piece, step, side, j).wait_recv()
                core_copy(piece, step, side, j, core).start()

    turns = [*range(len(PIECES))] + [int(n) for n in ORDER]
    progress = [0] * len(PIECES)
    for piece in turns + [n for n in range(len(PIECES)) for _ in range(longest)]:
        step = progress[piece]
        if step > len(steps[piece]):
            continue
        if step > 0:
            receive(piece, step - 1)
        if step < len(steps[piece]):
            start(piece, step)
        progress[piece] = step + 1
        if step == 0 and piece == len(PIECES) - 1:
            own_copy(core).start()
    own_copy(core).wait_send()
    own_copy(1 - core).wait_recv()
    for piece in range(len(PIECES)):
        for step in range(len(steps[piece])):
            for side in (1, -1):
                j, goes = sends(piece, step, side)

                @pl.when(goes)
                def _(j=j, side=side, piece=piece, step=step):
                    line_copy(piece, step, side, j).wait_send()

                j, comes = arrives(piece, step, side)

                @pl.when(comes)
                def _(j=j, side=side, piece=piece, step=step):
                    core_copy(piece, step, side, j, core).wait_send()
                    core_copy(piece, step, side, j, 1 - core).wait_recv()


def gather(offered):
    sizes = line_sizes()
    slots = len(PIECES) * sum(n - 1 for n in sizes) * 2
    return pl.pallas_call(
        functools.partial(gather_kernel, sizes),
        out_shape=jax.ShapeDtypeStruct((sizes[0], 2, sizes[1], sizes[2], ROWS, LANES), jnp.float32),
        in_specs=[VMEM],
        out_specs=VMEM,
        scratch_shapes=[pltpu.SemaphoreType.DMA((slots,))] * 4 + [pltpu.SemaphoreType.DMA] * 2,
        compiler_params=pltpu.CompilerParams(
            collective_id=0, has_side_effects=True, vmem_limit_bytes=48 * 1024 * 1024
        ),
        name="gather",
    )(offered)


def table_kernel(capacity, me_ref, rows_ref, out_ref):
    domains = rows_ref.shape[0]
    rows = rows_ref[...]
    payload = jnp.concatenate([rows[d, 0:1, :] for d in range(domains)], axis=0)
    owner = jnp.concatenate([rows[d, 1:2, :] for d in range(domains)], axis=0)
    mine = owner == me_ref[0].astype(jnp.float32)
    before = lax.broadcasted_iota(jnp.int32, (TILES_DEV, TILES_DEV), 0)
    after = lax.broadcasted_iota(jnp.int32, (TILES_DEV, TILES_DEV), 1)
    earlier = (before < after).astype(jnp.float32).astype(jnp.bfloat16)
    rank = jnp.dot(
        mine.astype(jnp.float32).astype(jnp.bfloat16), earlier, preferred_element_type=jnp.float32
    )
    lane = lax.broadcasted_iota(jnp.int32, (domains, TILES_DEV), 1)
    table = jnp.full((domains, TILES_DEV), -1.0, jnp.float32)
    for r in range(capacity):
        chosen = jnp.where(mine & (rank == float(r)), payload + 1.0, 0.0)
        chosen = jnp.sum(chosen, axis=1, keepdims=True) - 1.0
        table = jnp.where(lane == r, chosen, table)
    out_ref[...] = table.astype(jnp.int32)


def tile_kernel(
    capacity,
    table_ref,
    centers_ref,
    widths_ref,
    charges_ref,
    coords_ref,
    lanes_ref,
    planes_ref,
    out_ref,
    list_ref,
    total_ref,
):
    domains = table_ref.shape[0]
    total_ref[...] = jnp.zeros_like(total_ref)

    def collect(d, found):
        for r in range(capacity):
            entry = table_ref[d, r]
            list_ref[found] = entry
            found = found + (entry >= 0).astype(jnp.int32)
        return found

    found = lax.fori_loop(0, domains, collect, jnp.int32(0))
    list_ref[found] = 0

    def tile(j):
        entry = list_ref[j]
        source = lax.shift_right_logical(entry, 4)
        local = lax.bitwise_and(entry, CL_DEV - 1)
        home = lax.shift_right_logical(source, 4)
        within = lax.bitwise_and(source, CL_DEV - 1)
        return entry, source, local, home, within

    def one_tile(j, me):
        _, source, local, home, within = tile(j)
        target = me * CL_DEV + local
        scale = jnp.where(j < found, jnp.float32(biot_factor), jnp.float32(0.0))
        width_t = widths_ref[target]
        width_s = widths_ref[source]
        shift = [centers_ref[i, target] - centers_ref[i, source] for i in range(3)]
        first_row = lax.shift_right_logical(within, 1) * 24 + lax.bitwise_and(within, 1) * 4
        charge = [
            jnp.concatenate(
                [charges_ref[home, pl.ds(first_row + i * 8 + g, 1), :] for g in range(GROUPS)], axis=1
            )
            for i in range(3)
        ]
        unit = [lanes_ref[i : i + 1, :] for i in range(3)]
        near = [width_s * unit[i] for i in range(3)]
        moment = [
            near[1] * charge[2] - near[2] * charge[1],
            near[2] * charge[0] - near[0] * charge[2],
            near[0] * charge[1] - near[1] * charge[0],
        ]
        nothing = jnp.zeros((2, PROXIES), jnp.float32)
        features = jnp.concatenate(charge + moment + [nothing], axis=0)
        rest = features - features.astype(jnp.bfloat16).astype(jnp.float32)
        features = jnp.concatenate([features, rest], axis=0).astype(jnp.bfloat16)
        place = [width_t * unit[i] + shift[i] for i in range(3)]
        along_x = place[0] - width_s * lanes_ref[8:16, :]
        along_x = along_x * along_x
        along_y = place[1][:, :LANES] - width_s * planes_ref[:, :LANES]
        along_z = place[2][:, :LANES] - width_s * planes_ref[:, LANES:]
        plane = along_y * along_y + along_z * along_z + smoothing_sq
        summed = jnp.zeros((16, PROXIES), jnp.float32)
        for half in range(2):
            blocks = []
            for a in range(half * 4, half * 4 + 4):
                radius_sq = jnp.concatenate(
                    [plane + along_x[a : a + 1, g * LANES : (g + 1) * LANES] for g in range(GROUPS)], axis=1
                )
                inverse = lax.rsqrt(radius_sq)
                blocks.append(inverse * inverse * inverse)
            high, low = split(jnp.concatenate(blocks, axis=0))
            part = features[:, half * 256 : (half + 1) * 256]
            summed = summed + jnp.dot(part, high, preferred_element_type=jnp.float32)
            summed = summed + jnp.dot(part, low, preferred_element_type=jnp.float32)
        both = (summed[:8] + summed[8:]) * scale
        s = [both[i : i + 1] for i in range(6)]
        velocity = [
            place[1] * s[2] - place[2] * s[1] - s[3],
            place[2] * s[0] - place[0] * s[2] - s[4],
            place[0] * s[1] - place[1] * s[0] - s[5],
        ]
        return local, velocity

    me = lax.axis_index(AXES)

    def some_tiles(count, i, carry):
        for local, velocity in [one_tile(count * i + n, me) for n in range(count)]:
            for n in range(3):
                total_ref[local, n : n + 1, :] += velocity[n]
        return carry

    fours = lax.shift_right_logical(found, 2)
    lax.fori_loop(0, fours, functools.partial(some_tiles, 4), 0)
    lax.fori_loop(2 * fours, lax.shift_right_logical(found + 1, 1), functools.partial(some_tiles, 2), 0)

    basis = basis_columns(range(NODES))

    def down(c):
        at = pl.ds(pl.multiple_of(c * PTS, PTS), PTS)
        basis_x = lagrange(coords_ref[0:1, at], basis)
        basis_y = lagrange(coords_ref[1:2, at], basis)
        basis_z = lagrange(coords_ref[2:3, at], basis)
        high, low = split(paired_basis(basis_y, basis_z))
        values = total_ref[c]
        values = jnp.concatenate([values[:, a * PLANE : (a + 1) * PLANE] for a in range(NODES)], axis=0)
        values_high, values_low = split(values)
        left = jnp.concatenate([values_high, values_low, values_high], axis=1)
        right = jnp.concatenate([high, high, low], axis=0)
        spread = jnp.dot(left, right, preferred_element_type=jnp.float32)
        velocity = basis_x[0:1, :] * spread[0:8]
        for a in range(1, NODES):
            velocity = velocity + basis_x[a : a + 1, :] * spread[a * 8 : (a + 1) * 8]
        out_ref[:, at] = velocity[:3]

    def two_down(p, carry):
        down(2 * p)
        down(2 * p + 1)
        return carry

    lax.fori_loop(0, CL_DEV // 2, two_down, 0)


def local(point_coords, strengths, centers, half_widths, tile_source, tile_target, tile_count):
    domains = lax.axis_size(AXES)
    capacity = (TILES_DEV + domains - 1) // domains
    params = pltpu.CompilerParams(vmem_limit_bytes=48 * 1024 * 1024)

    def whole(*shape):
        return pl.BlockSpec(shape, lambda i: (0,) * len(shape))

    offered = pl.pallas_call(
        up_kernel,
        grid=(1,),
        out_shape=jax.ShapeDtypeStruct((ROWS, LANES), jnp.float32),
        in_specs=[SMEM]
        + [whole(3, CL_DEV * PTS), whole(3, CL_DEV * PTS), whole(1, TILES_DEV), whole(1, TILES_DEV)],
        out_specs=whole(ROWS, LANES),
        compiler_params=params,
        name="upward",
    )(tile_count, point_coords, strengths, tile_source, tile_target)
    gathered = gather(offered).reshape(domains, ROWS, LANES)
    me = lax.axis_index(AXES).astype(jnp.int32).reshape(1)
    table = pl.pallas_call(
        functools.partial(table_kernel, capacity),
        grid=(1,),
        out_shape=jax.ShapeDtypeStruct((domains, TILES_DEV), jnp.int32),
        in_specs=[SMEM, pl.BlockSpec((domains, 8, LANES), lambda i: (0, CHARGE_ROWS // 8, 0))],
        out_specs=pl.BlockSpec((domains, TILES_DEV), lambda i: (0, 0)),
        compiler_params=params,
        name="tables",
    )(me, gathered)
    return pl.pallas_call(
        functools.partial(tile_kernel, capacity),
        out_shape=jax.ShapeDtypeStruct((3, CL_DEV * PTS), jnp.float32),
        in_specs=[SMEM] * 3 + [VMEM] * 4,
        out_specs=VMEM,
        scratch_shapes=[
            pltpu.SMEM((domains * capacity + 8,), jnp.int32),
            pltpu.VMEM((CL_DEV, 8, PROXIES), jnp.float32),
        ],
        compiler_params=params,
        name="tiles",
    )(
        table,
        centers,
        half_widths,
        gathered,
        point_coords,
        jnp.asarray(lane_tables()),
        jnp.asarray(plane_tables()),
    )


def solution(mesh):
    return jax.shard_map(
        local,
        mesh=mesh,
        in_specs=(
            P(None, AXES),
            P(None, AXES),
            P(),
            P(),
            P(AXES, None),
            P(AXES, None),
            P(AXES),
        ),
        out_specs=P(None, AXES),
        check_vma=False,
    )
```

```python
import functools

import jax
import jax.numpy as jnp
import numpy as np
from jax import lax
from jax.experimental import pallas as pl
from jax.experimental.pallas import tpu as pltpu
from jax.sharding import PartitionSpec as P

CL_DEV = 16
PTS = 1024
DEG = 7
TILES_DEV = 128
AXES = ("gx", "gy")

NODES = DEG + 1
PLANE = NODES * NODES
PROXIES = NODES**3
LANES = 128
GROUPS = PROXIES // LANES
CHARGE_ROWS = CL_DEV * 3 * GROUPS
ROWS = CHARGE_ROWS + 8
smoothing_sq = 0.01
biot_factor = -0.07957747154594767

CHEB = np.cos(np.pi * np.arange(NODES) / DEG)
EVEN_ODD = [0, 2, 4, 6, 1, 3, 5, 7]
VMEM = pl.BlockSpec(memory_space=pltpu.VMEM)
SMEM = pl.BlockSpec(memory_space=pltpu.SMEM)


def basis_columns(order):
    row = lax.broadcasted_iota(jnp.int32, (NODES, LANES), 0)

    def column(values):
        tile = jnp.full((NODES, LANES), float(values[0]), jnp.float32)
        for n in range(1, NODES):
            tile = jnp.where(row == n, jnp.float32(values[n]), tile)
        return tile

    others = [[m for m in range(NODES) if m != a] for a in order]
    columns = [column([CHEB[left[j]] for left in others]) for j in range(DEG)]
    inverse = [1.0 / np.prod([CHEB[a] - CHEB[m] for m in left]) for a, left in zip(order, others)]
    return columns + [column(inverse)]


def lane_tables():
    k = np.arange(PROXIES)
    table = np.zeros((16, PROXIES), np.float32)
    table[0] = CHEB[k // PLANE]
    table[1] = CHEB[(k // NODES) % NODES]
    table[2] = CHEB[k % NODES]
    table[8:16] = CHEB[:, None]
    return table


def plane_tables():
    rows = np.arange(PLANE)
    along_y = np.repeat(CHEB[rows // NODES][:, None], LANES, axis=1)
    along_z = np.repeat(CHEB[rows % NODES][:, None], LANES, axis=1)
    return np.concatenate([along_y, along_z], axis=1).astype(np.float32)


def lagrange(row, columns):
    repeats = row.shape[1] // LANES

    def column(j):
        return jnp.concatenate([columns[j]] * repeats, axis=1)

    value = (row - column(0)) * column(DEG)
    for j in range(1, DEG):
        value = value * (row - column(j))
    return value


def split(value):
    high = value.astype(jnp.bfloat16)
    low = (value - high.astype(jnp.float32)).astype(jnp.bfloat16)
    return high, low


def paired_basis(basis_y, basis_z):
    return jnp.concatenate([basis_y[b : b + 1, :] * basis_z for b in range(NODES)], axis=0)


def up_kernel(count_ref, coords_ref, weights_ref, source_ref, target_ref, out_ref):
    basis = basis_columns(range(NODES))
    mixed = basis_columns(EVEN_ODD)
    lane = lax.broadcasted_iota(jnp.int32, (NODES, LANES), 1)
    row = lax.broadcasted_iota(jnp.int32, (NODES, LANES), 0)
    low_lanes = lane < PLANE

    def cluster(c):
        at = pl.ds(pl.multiple_of(c * PTS, PTS), PTS)
        basis_x = lagrange(coords_ref[0:1, at], mixed)
        basis_y = lagrange(coords_ref[1:2, at], basis)
        basis_z = lagrange(coords_ref[2:3, at], basis)
        left = jnp.concatenate([weights_ref[i : i + 1, at] * basis_x for i in range(3)], axis=0)
        left_rest = left - left.astype(jnp.bfloat16).astype(jnp.float32)
        left = jnp.concatenate([left, left_rest], axis=0).astype(jnp.bfloat16)
        right = jnp.concatenate(split(paired_basis(basis_y, basis_z)), axis=0)
        product = lax.dot_general(
            left, right, (((1,), (1,)), ((), ())), preferred_element_type=jnp.float32
        )
        both = product[: 3 * NODES] + product[3 * NODES :]
        return both + pltpu.roll(both, PLANE, 1)

    def pair(p, carry):
        first = cluster(2 * p)
        second = cluster(2 * p + 1)
        for i in range(3):
            one = first[i * NODES : (i + 1) * NODES]
            two = second[i * NODES : (i + 1) * NODES]
            one = jnp.where(low_lanes, one, pltpu.roll(one, 4, 0))
            two = jnp.where(low_lanes, pltpu.roll(two, 4, 0), two)
            at = pl.ds(pl.multiple_of(p * 24 + i * 8, 8), 8)
            out_ref[at, :] = jnp.where(row < 4, one, two)
        return carry

    lax.fori_loop(0, CL_DEV // 2, pair, 0)
    source = source_ref[...]
    target = target_ref[...]
    owner = lax.shift_right_logical(target, 4)
    payload = (source * CL_DEV + (target - owner * CL_DEV)).astype(jnp.float32)
    alive = lax.broadcasted_iota(jnp.int32, (1, TILES_DEV), 1) < count_ref[0]
    owner = jnp.where(alive, owner, -1).astype(jnp.float32)
    out_ref[CHARGE_ROWS:, :] = jnp.where(row == 0, payload, jnp.where(row == 1, owner, 0.0))


PIECES = (
    (0, 80, (1, 0, 2)),
    (80, 64, (2, 1, 0)),
    (144, 56, (0, 2, 1)),
)
ORDER = "010210210212"


def line_sizes():
    along_x = lax.axis_size("gx") // 2
    minor = lax.axis_size("gy")
    fast = max(n for n in range(1, minor + 1) if minor % n == 0 and n * n <= minor)
    return (along_x, minor // fast, fast)


def gather_kernel(sizes, offered_ref, out_ref, line_send, line_recv, core_send, core_recv):
    major = lax.axis_index("gx")
    minor = lax.axis_index("gy")
    core = lax.rem(major, 2)
    at = (major // 2, minor // sizes[2], lax.rem(minor, sizes[2]))
    partner = (major + 1 - 2 * core, minor)

    def device(axis, by):
        spot = list(at)
        spot[axis] = spot[axis] + by
        return (spot[0] * 2 + core, spot[1] * sizes[2] + spot[2])

    steps = [[(axis, s) for axis in order for s in range(sizes[axis] - 1)] for _, _, order in PIECES]
    longest = max(len(s) for s in steps)

    def chunk(piece, step, j, of_core):
        first, count, order = PIECES[piece]
        axis = steps[piece][step][0]
        done = order[: order.index(axis)]
        spot = [slice(None) if n in done else (j if n == axis else at[n]) for n in range(3)]
        return out_ref.at[spot[0], of_core, spot[1], spot[2], pl.ds(first, count), :]

    def line_copy(piece, step, side, j):
        slot = (piece * longest + step) * 2 + (1 if side > 0 else 0)
        ref = chunk(piece, step, j, core)
        return pltpu.make_async_remote_copy(
            src_ref=ref,
            dst_ref=ref,
            send_sem=line_send.at[slot],
            recv_sem=line_recv.at[slot],
            device_id=device(steps[piece][step][0], side),
            device_id_type=pl.DeviceIdType.MESH,
        )

    def core_copy(ref):
        return pltpu.make_async_remote_copy(
            src_ref=ref,
            dst_ref=ref,
            send_sem=core_send,
            recv_sem=core_recv,
            device_id=partner,
            device_id_type=pl.DeviceIdType.MESH,
        )

    def sends(piece, step, side):
        axis, s = steps[piece][step]
        j = at[axis] - side * s
        goes = (j >= 0) & (j < sizes[axis]) & (at[axis] + side >= 0) & (at[axis] + side < sizes[axis])
        return j, goes

    def arrives(piece, step, side):
        axis, s = steps[piece][step]
        j = at[axis] - side * (s + 1)
        return j, (j >= 0) & (j < sizes[axis])

    barrier = pltpu.get_barrier_semaphore()
    expected = jnp.int32(1)
    pl.semaphore_signal(barrier, inc=1, device_id=partner, device_id_type=pl.DeviceIdType.MESH)
    for axis in range(3):
        for side in (1, -1):
            there = (at[axis] + side >= 0) & (at[axis] + side < sizes[axis])
            expected = expected + there.astype(jnp.int32)

            @pl.when(there)
            def _(axis=axis, side=side):
                pl.semaphore_signal(
                    barrier, inc=1, device_id=device(axis, side), device_id_type=pl.DeviceIdType.MESH
                )

    out_ref[at[0], core, at[1], at[2]] = offered_ref[...]
    pl.semaphore_wait(barrier, expected)

    def start(piece, step):
        for side in (1, -1):
            j, goes = sends(piece, step, side)

            @pl.when(goes)
            def _(j=j, side=side):
                line_copy(piece, step, side, j).start()

    def receive(piece, step):
        for side in (1, -1):
            j, comes = arrives(piece, step, side)

            @pl.when(comes)
            def _(j=j, side=side):
                line_copy(piece, step, side, j).wait_recv()
                core_copy(chunk(piece, step, j, core)).start()

    turns = [*range(len(PIECES))] + [int(n) for n in ORDER]
    progress = [0] * len(PIECES)
    for piece in turns + [n for n in range(len(PIECES)) for _ in range(longest)]:
        step = progress[piece]
        if step > len(steps[piece]):
            continue
        if step > 0:
            receive(piece, step - 1)
        if step < len(steps[piece]):
            start(piece, step)
        progress[piece] = step + 1
        if step == 0 and piece == len(PIECES) - 1:
            core_copy(out_ref.at[at[0], core, at[1], at[2]]).start()
    core_copy(out_ref.at[:, core]).wait_send()
    core_copy(out_ref.at[:, 1 - core]).wait_recv()
    for piece in range(len(PIECES)):
        for step in range(len(steps[piece])):
            for side in (1, -1):
                j, goes = sends(piece, step, side)

                @pl.when(goes)
                def _(j=j, side=side, piece=piece, step=step):
                    line_copy(piece, step, side, j).wait_send()


def gather(offered):
    sizes = line_sizes()
    slots = len(PIECES) * sum(n - 1 for n in sizes) * 2
    return pl.pallas_call(
        functools.partial(gather_kernel, sizes),
        out_shape=jax.ShapeDtypeStruct((sizes[0], 2, sizes[1], sizes[2], ROWS, LANES), jnp.float32),
        in_specs=[VMEM],
        out_specs=VMEM,
        scratch_shapes=[pltpu.SemaphoreType.DMA((slots,))] * 2 + [pltpu.SemaphoreType.DMA] * 2,
        compiler_params=pltpu.CompilerParams(
            collective_id=0, has_side_effects=True, vmem_limit_bytes=48 * 1024 * 1024
        ),
        name="gather",
    )(offered)


def table_kernel(capacity, me_ref, rows_ref, out_ref):
    domains = rows_ref.shape[0]
    rows = rows_ref[...]
    payload = jnp.concatenate([rows[d, 0:1, :] for d in range(domains)], axis=0)
    owner = jnp.concatenate([rows[d, 1:2, :] for d in range(domains)], axis=0)
    mine = owner == me_ref[0].astype(jnp.float32)
    before = lax.broadcasted_iota(jnp.int32, (TILES_DEV, TILES_DEV), 0)
    after = lax.broadcasted_iota(jnp.int32, (TILES_DEV, TILES_DEV), 1)
    earlier = (before < after).astype(jnp.float32).astype(jnp.bfloat16)
    rank = jnp.dot(
        mine.astype(jnp.float32).astype(jnp.bfloat16), earlier, preferred_element_type=jnp.float32
    )
    lane = lax.broadcasted_iota(jnp.int32, (domains, TILES_DEV), 1)
    table = jnp.full((domains, TILES_DEV), -1.0, jnp.float32)
    for r in range(capacity):
        chosen = jnp.where(mine & (rank == float(r)), payload + 1.0, 0.0)
        chosen = jnp.sum(chosen, axis=1, keepdims=True) - 1.0
        table = jnp.where(lane == r, chosen, table)
    out_ref[...] = table.astype(jnp.int32)


def tile_kernel(
    capacity,
    table_ref,
    centers_ref,
    widths_ref,
    charges_ref,
    coords_ref,
    lanes_ref,
    planes_ref,
    out_ref,
    list_ref,
    total_ref,
):
    domains = table_ref.shape[0]
    total_ref[...] = jnp.zeros_like(total_ref)

    def collect(d, found):
        for r in range(capacity):
            entry = table_ref[d, r]
            list_ref[found] = entry
            found = found + (entry >= 0).astype(jnp.int32)
        return found

    found = lax.fori_loop(0, domains, collect, jnp.int32(0))
    list_ref[found] = 0

    def tile(j):
        entry = list_ref[j]
        source = lax.shift_right_logical(entry, 4)
        local = lax.bitwise_and(entry, CL_DEV - 1)
        home = lax.shift_right_logical(source, 4)
        within = lax.bitwise_and(source, CL_DEV - 1)
        return entry, source, local, home, within

    def one_tile(j, me):
        _, source, local, home, within = tile(j)
        target = me * CL_DEV + local
        scale = jnp.where(j < found, jnp.float32(biot_factor), jnp.float32(0.0))
        width_t = widths_ref[target]
        width_s = widths_ref[source]
        shift = [centers_ref[i, target] - centers_ref[i, source] for i in range(3)]
        first_row = lax.shift_right_logical(within, 1) * 24 + lax.bitwise_and(within, 1) * 4
        charge = [
            jnp.concatenate(
                [charges_ref[home, pl.ds(first_row + i * 8 + g, 1), :] for g in range(GROUPS)], axis=1
            )
            for i in range(3)
        ]
        unit = [lanes_ref[i : i + 1, :] for i in range(3)]
        near = [width_s * unit[i] for i in range(3)]
        moment = [
            near[1] * charge[2] - near[2] * charge[1],
            near[2] * charge[0] - near[0] * charge[2],
            near[0] * charge[1] - near[1] * charge[0],
        ]
        nothing = jnp.zeros((2, PROXIES), jnp.float32)
        features = jnp.concatenate(charge + moment + [nothing], axis=0)
        rest = features - features.astype(jnp.bfloat16).astype(jnp.float32)
        features = jnp.concatenate([features, rest], axis=0).astype(jnp.bfloat16)
        place = [width_t * unit[i] + shift[i] for i in range(3)]
        along_x = place[0] - width_s * lanes_ref[8:16, :]
        along_x = along_x * along_x
        along_y = place[1][:, :LANES] - width_s * planes_ref[:, :LANES]
        along_z = place[2][:, :LANES] - width_s * planes_ref[:, LANES:]
        plane = along_y * along_y + along_z * along_z + smoothing_sq
        summed = jnp.zeros((16, PROXIES), jnp.float32)
        for half in range(2):
            blocks = []
            for a in range(half * 4, half * 4 + 4):
                radius_sq = jnp.concatenate(
                    [plane + along_x[a : a + 1, g * LANES : (g + 1) * LANES] for g in range(GROUPS)], axis=1
                )
                inverse = lax.rsqrt(radius_sq)
                blocks.append(inverse * inverse * inverse)
            high, low = split(jnp.concatenate(blocks, axis=0))
            part = features[:, half * 256 : (half + 1) * 256]
            summed = summed + jnp.dot(part, high, preferred_element_type=jnp.float32)
            summed = summed + jnp.dot(part, low, preferred_element_type=jnp.float32)
        both = (summed[:8] + summed[8:]) * scale
        s = [both[i : i + 1] for i in range(6)]
        velocity = [
            place[1] * s[2] - place[2] * s[1] - s[3],
            place[2] * s[0] - place[0] * s[2] - s[4],
            place[0] * s[1] - place[1] * s[0] - s[5],
        ]
        return local, velocity

    me = lax.axis_index(AXES)

    def some_tiles(count, i, carry):
        for local, velocity in [one_tile(count * i + n, me) for n in range(count)]:
            for n in range(3):
                total_ref[local, n : n + 1, :] += velocity[n]
        return carry

    fours = lax.shift_right_logical(found, 2)
    lax.fori_loop(0, fours, functools.partial(some_tiles, 4), 0)
    lax.fori_loop(2 * fours, lax.shift_right_logical(found + 1, 1), functools.partial(some_tiles, 2), 0)

    basis = basis_columns(range(NODES))

    def down(c):
        at = pl.ds(pl.multiple_of(c * PTS, PTS), PTS)
        basis_x = lagrange(coords_ref[0:1, at], basis)
        basis_y = lagrange(coords_ref[1:2, at], basis)
        basis_z = lagrange(coords_ref[2:3, at], basis)
        high, low = split(paired_basis(basis_y, basis_z))
        values = total_ref[c]
        values = jnp.concatenate([values[:, a * PLANE : (a + 1) * PLANE] for a in range(NODES)], axis=0)
        values_high, values_low = split(values)
        left = jnp.concatenate([values_high, values_low, values_high], axis=1)
        right = jnp.concatenate([high, high, low], axis=0)
        spread = jnp.dot(left, right, preferred_element_type=jnp.float32)
        velocity = basis_x[0:1, :] * spread[0:8]
        for a in range(1, NODES):
            velocity = velocity + basis_x[a : a + 1, :] * spread[a * 8 : (a + 1) * 8]
        out_ref[:, at] = velocity[:3]

    def two_down(p, carry):
        down(2 * p)
        down(2 * p + 1)
        return carry

    lax.fori_loop(0, CL_DEV // 2, two_down, 0)


def local(point_coords, strengths, centers, half_widths, tile_source, tile_target, tile_count):
    domains = lax.axis_size(AXES)
    capacity = (TILES_DEV + domains - 1) // domains
    params = pltpu.CompilerParams(vmem_limit_bytes=48 * 1024 * 1024)

    def whole(*shape):
        return pl.BlockSpec(shape, lambda i: (0,) * len(shape))

    offered = pl.pallas_call(
        up_kernel,
        grid=(1,),
        out_shape=jax.ShapeDtypeStruct((ROWS, LANES), jnp.float32),
        in_specs=[SMEM]
        + [whole(3, CL_DEV * PTS), whole(3, CL_DEV * PTS), whole(1, TILES_DEV), whole(1, TILES_DEV)],
        out_specs=whole(ROWS, LANES),
        compiler_params=params,
        name="upward",
    )(tile_count, point_coords, strengths, tile_source, tile_target)
    gathered = gather(offered).reshape(domains, ROWS, LANES)
    me = lax.axis_index(AXES).astype(jnp.int32).reshape(1)
    table = pl.pallas_call(
        functools.partial(table_kernel, capacity),
        grid=(1,),
        out_shape=jax.ShapeDtypeStruct((domains, TILES_DEV), jnp.int32),
        in_specs=[SMEM, pl.BlockSpec((domains, 8, LANES), lambda i: (0, CHARGE_ROWS // 8, 0))],
        out_specs=pl.BlockSpec((domains, TILES_DEV), lambda i: (0, 0)),
        compiler_params=params,
        name="tables",
    )(me, gathered)
    return pl.pallas_call(
        functools.partial(tile_kernel, capacity),
        out_shape=jax.ShapeDtypeStruct((3, CL_DEV * PTS), jnp.float32),
        in_specs=[SMEM] * 3 + [VMEM] * 4,
        out_specs=VMEM,
        scratch_shapes=[
            pltpu.SMEM((domains * capacity + 8,), jnp.int32),
            pltpu.VMEM((CL_DEV, 8, PROXIES), jnp.float32),
        ],
        compiler_params=params,
        name="tiles",
    )(
        table,
        centers,
        half_widths,
        gathered,
        point_coords,
        jnp.asarray(lane_tables()),
        jnp.asarray(plane_tables()),
    )


def solution(mesh):
    return jax.shard_map(
        local,
        mesh=mesh,
        in_specs=(
            P(None, AXES),
            P(None, AXES),
            P(),
            P(),
            P(AXES, None),
            P(AXES, None),
            P(AXES),
        ),
        out_specs=P(None, AXES),
        check_vma=False,
    )
```
